32 devices in a mesh: seq: 16 (over z, y, core), head: 2 (over x).
Axes of the slice: x: 2, y: 2, z: 4, core: 2. Of those that a mesh axis runs over, the one named last changes fastest.
Arguments:
- queries: bfloat16 [16384, 2048], P('seq', 'head'), may hold values from -8 to 8
- key_states: bfloat16 [16384, 2048], P('seq', 'head'), may hold values from -8 to 8
- value_states: bfloat16 [16384, 2048], P('seq', 'head'), may hold values from -6 to 6
- out_weight: bfloat16 [2048, 2048], P('head'), may hold values from -0.125 to 0.125
- cotangent: bfloat16 [16384, 2048], P('seq', 'head'), may hold values from -6 to 6
Outputs:
- attended: bfloat16 [16384, 2048], P('seq', 'head')
- grad_queries: bfloat16 [16384, 2048], P('seq', 'head')
- grad_keys: bfloat16 [16384, 2048], P('seq', 'head')
- grad_values: bfloat16 [16384, 2048], P('seq', 'head')
- grad_weight: bfloat16 [2048, 2048], P('head')
The draws below stay inside these ranges and needn't reach their ends.
All inputs are finite; a program needn't handle non-finite values.
Results may differ from the reference program's by a relative error of at most 0.02.
Values may be sent and summed in bfloat16 or wider, within the bound.
No kernel may reach another device: no remote copies, remote signals or barrier semaphores. Data moves between devices by JAX's collectives and lax.ppermute only.
A program may use at most 256 MiB of HBM per device.

```python
import jax
import jax.numpy as jnp
from jax import lax

HEADS = 16
HEAD_DIM = 128
BLOCK = 256
POOLED = 128
D = 2048
HEADS_DEV = 8
SEQ = 16384
N_HEAD = 2


def base_draw(key):
    return jnp.clip(jax.random.normal(key, (SEQ, D), jnp.float32), -6.0, 6.0)


def draw_queries(key, part):
    values = base_draw(jax.random.fold_in(key, 1))
    return values.astype(jnp.bfloat16)


def draw_key_states(key, part):
    values = base_draw(jax.random.fold_in(key, 2))
    return values.astype(jnp.bfloat16)


def level_of(stream_key, dims, split, smallest, largest):
    level, own = 1.0, jax.random.fold_in(stream_key, 6)
    for dim, blocks in split:
        heights = jnp.exp(jax.random.uniform(jax.random.fold_in(own, dim), (blocks,), jnp.float32, smallest / len(split), largest / len(split)))
        level = level * jnp.repeat(heights, dims[dim] // blocks).reshape([-1 if axis == dim else 1 for axis in range(len(dims))])
    return level


def bell_draw(rng, dims, deviation, most, shards=(), kind=jnp.bfloat16):
    result = jax.random.normal(rng, dims, jnp.float32) * deviation
    if len(shards) > 0:
        result = level_of(rng, dims, shards, -0.22, 0.18) * result
    return jnp.clip(result, min=-most, max=most).astype(kind)


def setup_inputs(seed: int = 0) -> dict:
    streams_of = jax.random.split(jax.random.key(seed), 6)
    queries = draw_queries(jax.random.fold_in(streams_of[5], 71), 0)
    key_states = draw_key_states(jax.random.fold_in(streams_of[5], 71), 0)
    value_states = bell_draw(streams_of[2], (SEQ, D), 1.0, 6.0, ((0, 16), (1, 2)))
    out_weight = bell_draw(streams_of[3], (D, D), D ** -0.5, 0.125, ((0, 2),))
    cotangent = bell_draw(streams_of[4], (SEQ, D), 1.0, 6.0, ((0, 16), (1, 2)))
    return {"queries": queries, "key_states": key_states, "value_states": value_states, "out_weight": out_weight, "cotangent": cotangent}


def pair_mean(rows):
    wide = rows.astype(jnp.float32).reshape(rows.shape[0] // 2, 2, rows.shape[1])
    return (0.5 * (wide[:, 0] + wide[:, 1])).astype(jnp.bfloat16)


def widen(rows):
    return jnp.repeat(rows, 2, axis=0) * 0.5


def rounded(values):
    return lax.optimization_barrier(values.astype(jnp.bfloat16)).astype(jnp.float32)


def sibling_rows(coarse, level):
    width = coarse.shape[1]
    halves = coarse.reshape(-1, 2, POOLED, width)[:, ::-1].reshape(-1, POOLED, width)
    return jnp.repeat(halves, 2 ** (level - 1), axis=0)


def sibling_grads(part, level):
    width = part.shape[2]
    span = 2 ** (level - 1)
    summed = jnp.sum(part.reshape(-1, span, POOLED, width), axis=1)
    return summed.reshape(-1, 2, POOLED, width)[:, ::-1].reshape(-1, width)


def head_pass(operands):
    query, key_rows, value_rows, grad_mixed = operands
    blocks = SEQ // BLOCK
    levels = blocks.bit_length() - 1
    logit_scale = HEAD_DIM ** -0.5
    key_parts = [key_rows.reshape(blocks, BLOCK, HEAD_DIM)]
    value_parts = [value_rows.reshape(blocks, BLOCK, HEAD_DIM)]
    coarse_keys = key_rows
    coarse_values = value_rows
    for level in range(1, levels + 1):
        coarse_keys = pair_mean(coarse_keys)
        coarse_values = pair_mean(coarse_values)
        key_parts.append(sibling_rows(coarse_keys, level))
        value_parts.append(sibling_rows(coarse_values, level))
    gathered_key_rows = jnp.concatenate(key_parts, axis=1).astype(jnp.float32)
    gathered_value_rows = jnp.concatenate(value_parts, axis=1).astype(jnp.float32)
    blocked_queries = query.reshape(blocks, BLOCK, HEAD_DIM).astype(jnp.float32)
    attention_logits = logit_scale * jnp.einsum("ohw,oiw->ohi", blocked_queries, gathered_key_rows)
    top = jnp.max(attention_logits, axis=-1, keepdims=True)
    expo = jnp.exp(attention_logits - top)
    probs = expo / jnp.sum(expo, axis=-1, keepdims=True)
    attention_probabilities = rounded(probs)
    blended_output = jnp.einsum("xlv,xvd->xld", attention_probabilities, gathered_value_rows).astype(jnp.bfloat16)
    block_gradient_rows = grad_mixed.reshape(blocks, BLOCK, HEAD_DIM).astype(jnp.float32)
    probability_gradient = jnp.einsum("ohw,oiw->ohi", block_gradient_rows, gathered_value_rows)
    inner = jnp.sum(probs * probability_gradient, axis=-1, keepdims=True)
    logit_gradient = rounded(probs * (probability_gradient - inner))
    query_gradient = (logit_scale * jnp.einsum("xlv,xvd->xld", logit_gradient, gathered_key_rows)).astype(jnp.bfloat16)
    gathered_key_gradient = logit_scale * jnp.einsum("ozj,ozc->ojc", logit_gradient, blocked_queries)
    gathered_value_gradient = jnp.einsum("ozj,ozc->ojc", attention_probabilities, block_gradient_rows)
    accum_keys = None
    accum_values = None
    for level in range(levels, 0, -1):
        offset = BLOCK + (level - 1) * POOLED
        back_keys = sibling_grads(gathered_key_gradient[:, offset:offset + POOLED], level)
        back_values = sibling_grads(gathered_value_gradient[:, offset:offset + POOLED], level)
        if accum_keys is None:
            accum_keys = back_keys
            accum_values = back_values
        else:
            accum_keys = back_keys + widen(accum_keys)
            accum_values = back_values + widen(accum_values)
    grad_key = gathered_key_gradient[:, :BLOCK].reshape(SEQ, HEAD_DIM) + widen(accum_keys)
    grad_value = gathered_value_gradient[:, :BLOCK].reshape(SEQ, HEAD_DIM) + widen(accum_values)
    return (blended_output.reshape(SEQ, HEAD_DIM), query_gradient.reshape(SEQ, HEAD_DIM),
            grad_key.astype(jnp.bfloat16), grad_value.astype(jnp.bfloat16))


def by_head(values):
    return values.reshape(SEQ, HEADS, HEAD_DIM).transpose(1, 0, 2)


def to_rows(values):
    return values.transpose(1, 0, 2).reshape(SEQ, HEADS * HEAD_DIM)


def reference(queries, key_states, value_states, out_weight, cotangent):
    grad_mixed = jnp.dot(cotangent, out_weight.T, preferred_element_type=jnp.float32).astype(jnp.bfloat16)
    blended_output, query_gradient, grad_key, grad_value = lax.map(
        head_pass, (by_head(queries), by_head(key_states), by_head(value_states), by_head(grad_mixed)))
    blended_output = to_rows(blended_output)
    width = HEADS_DEV * HEAD_DIM
    total = jnp.zeros((SEQ, D), jnp.float32)
    for index in range(N_HEAD):
        partial_out = jnp.dot(blended_output[:, index * width:(index + 1) * width],
                              out_weight[index * width:(index + 1) * width],
                              preferred_element_type=jnp.float32)
        total = total + rounded(partial_out)
    attended = total.astype(jnp.bfloat16)
    grad_weight = jnp.dot(blended_output.T, cotangent, preferred_element_type=jnp.float32).astype(jnp.bfloat16)
    return attended, to_rows(query_gradient), to_rows(grad_key), to_rows(grad_value), grad_weight
```

```python
import functools

import jax
import jax.numpy as jnp
from jax import lax
from jax.experimental import pallas as pl
from jax.experimental.pallas import tpu as pltpu
from jax.sharding import PartitionSpec as P

HEAD_DIM = 128
BLOCK = 256
POOLED = 128
SCALE = HEAD_DIM ** -0.5
SCALE2 = SCALE * 1.4426950408889634
VMEM = 48 * 1024 * 1024
F32 = jnp.float32
BF16 = jnp.bfloat16


def params():
    return pltpu.CompilerParams(vmem_limit_bytes=VMEM)


def nn(a, b):
    return lax.dot_general(a, b, (((1,), (0,)), ((), ())), preferred_element_type=F32)


def nt(a, b):
    return lax.dot_general(a, b, (((1,), (1,)), ((), ())), preferred_element_type=F32)


def tn(a, b):
    return lax.dot_general(a, b, (((0,), (0,)), ((), ())), preferred_element_type=F32)


def pool_matrix(rows, columns):
    row = lax.broadcasted_iota(jnp.int32, (rows, columns), 0)
    column = lax.broadcasted_iota(jnp.int32, (rows, columns), 1)
    return jnp.where((column >> 1) == row, 0.5, 0.0).astype(BF16)


def widen_matrix(rows, columns, shift):
    row = lax.broadcasted_iota(jnp.int32, (rows, columns), 0)
    column = lax.broadcasted_iota(jnp.int32, (rows, columns), 1)
    return jnp.where((row >> shift) == column, 0.5 ** shift, 0.0).astype(BF16)


def from_partner(block, bit):
    count = lax.axis_size("seq")
    return lax.ppermute(block, "seq", [(low, low ^ 1 << bit) for low in range(count)])


def pool_kernel(local, cross, key_ref, value_ref, coarse_ref, summary_ref, pack_ref):
    big = pool_matrix(POOLED, BLOCK)
    small = pool_matrix(POOLED, POOLED)
    for index, ref in enumerate((key_ref, value_ref)):
        rows = ref[...]
        offset = 0
        for level in range(1, local + 1):
            parts = [
                nn(big, rows[start : start + BLOCK]) for start in range(0, rows.shape[0], BLOCK)
            ]
            rows = jnp.concatenate(parts, axis=0).astype(BF16)
            if level < local:
                coarse_ref[index, offset : offset + rows.shape[0], :] = rows
                offset += rows.shape[0]
        summary_ref[index] = rows
        pieces = []
        left = POOLED
        for bit in range(1, cross):
            wide = nn(small, rows)
            rows = wide.astype(BF16)
            pieces.append(wide[: POOLED >> bit])
            left -= POOLED >> bit
        pieces.append(jnp.zeros((left, rows.shape[1]), F32))
        pack_ref[index] = jnp.concatenate(pieces, axis=0).astype(BF16)


def pool(key_states, value_states, local, cross):
    rows, features = key_states.shape
    width = min(features, 256)
    total = sum(rows >> level for level in range(1, local))

    def spec(count):
        return pl.BlockSpec((2, count, width), lambda j: (0, 0, j))

    return pl.pallas_call(
        functools.partial(pool_kernel, local, cross),
        grid=(features // width,),
        in_specs=[pl.BlockSpec((rows, width), lambda j: (0, j))] * 2,
        out_specs=[spec(total), spec(POOLED), spec(POOLED)],
        out_shape=[
            jax.ShapeDtypeStruct((2, count, features), BF16) for count in (total, POOLED, POOLED)
        ],
        compiler_params=params(),
        name="pool",
    )(key_states, value_states)


def local_list(own, coarse, block, local, rows):
    parts = [own[block * BLOCK : (block + 1) * BLOCK]]
    offset = 0
    for level in range(1, local):
        sibling = block >> (level - 1) ^ 1
        start = offset + sibling * POOLED
        parts.append(coarse[start : start + POOLED])
        offset += rows >> level
    return jnp.concatenate(parts, axis=0)


def near_kernel(local, query_ref, key_ref, value_ref, coarse_ref, out_ref, stat_ref):
    rows = query_ref.shape[0]
    lane = lax.broadcasted_iota(jnp.int32, (BLOCK, HEAD_DIM), 1)
    for block in range(rows // BLOCK):
        here = slice(block * BLOCK, (block + 1) * BLOCK)
        keys = local_list(key_ref, coarse_ref.at[0], block, local, rows)
        values = local_list(value_ref, coarse_ref.at[1], block, local, rows)
        scores = nt(query_ref[here, :], keys)
        top = jnp.max(scores, axis=1, keepdims=True)
        weights = jnp.exp2((scores - top) * SCALE2)
        total = jnp.sum(weights, axis=1, keepdims=True)
        out_ref[here, :] = nn(weights.astype(BF16), values)
        stat_ref[here, :] = jnp.where(lane < 64, top, total)


def far_kernel(query_ref, first_ref, kept_ref, swapped_ref, near_ref, stat_ref, mixed_ref, lse_ref):
    rows = query_ref.shape[0]
    keys = jnp.concatenate([first_ref[0], kept_ref[0], swapped_ref[0]], axis=0)
    values = jnp.concatenate([first_ref[1], kept_ref[1], swapped_ref[1]], axis=0)
    for block in range(rows // BLOCK):
        here = slice(block * BLOCK, (block + 1) * BLOCK)
        scores = nt(query_ref[here, :], keys)
        near_top = stat_ref[here, 0:1]
        near_total = stat_ref[here, 64:65]
        top = jnp.maximum(near_top, jnp.max(scores, axis=1, keepdims=True))
        weights = jnp.exp2((scores - top) * SCALE2)
        shrink = jnp.exp2((near_top - top) * SCALE2)
        total = near_total * shrink + jnp.sum(weights, axis=1, keepdims=True)
        blend = near_ref[here, :] * shrink + nn(weights.astype(BF16), values)
        mixed_ref[here, :] = (blend / total).astype(BF16)
        lse = top * SCALE2 + jnp.log2(total)
        lse_ref[0, :, here] = jnp.broadcast_to(lse, (BLOCK, HEAD_DIM)).T[:8]


def column(rows):
    return pl.BlockSpec((rows, HEAD_DIM), lambda h: (0, h))


def pair(rows):
    return pl.BlockSpec((2, rows, HEAD_DIM), lambda h: (0, 0, h))


def row_stat(rows):
    return pl.BlockSpec((1, 8, rows), lambda h: (h, 0, 0))


def near_forward(queries, key_states, value_states, coarse, local):
    rows, features = queries.shape
    return pl.pallas_call(
        functools.partial(near_kernel, local),
        grid=(features // HEAD_DIM,),
        in_specs=[column(rows)] * 3 + [pair(coarse.shape[1])],
        out_specs=[column(rows)] * 2,
        out_shape=[jax.ShapeDtypeStruct((rows, features), F32)] * 2,
        compiler_params=params(),
        name="near_forward",
    )(queries, key_states, value_states, coarse)


def far_forward(queries, far, near, stat):
    rows, features = queries.shape
    heads = features // HEAD_DIM
    return pl.pallas_call(
        far_kernel,
        grid=(heads,),
        in_specs=[column(rows)] + [pair(part.shape[1]) for part in far] + [column(rows)] * 2,
        out_specs=[column(rows), row_stat(rows)],
        out_shape=[
            jax.ShapeDtypeStruct((rows, features), BF16),
            jax.ShapeDtypeStruct((heads, 8, rows), F32),
        ],
        compiler_params=params(),
        name="far_forward",
    )(queries, *far, near, stat)


def attend_back(queries, grad_mixed, keys, values, lse, inner):
    weights = jnp.exp2(nt(keys, queries) * SCALE2 - lse)
    grad_probs = nt(values, grad_mixed)
    grad_scores = (weights * (grad_probs - inner)).astype(BF16)
    grad_values = nn(weights.astype(BF16), grad_mixed)
    grad_keys = nn(grad_scores, queries)
    grad_queries = tn(grad_scores, keys)
    return grad_queries, grad_keys, grad_values


def far_back_kernel(
    query_ref, first_ref, kept_ref, swapped_ref, mixed_ref, grad_ref, lse_ref,
    grad_first_ref, grad_kept_ref, grad_swapped_ref, grad_query_ref, inner_ref,
):
    rows = query_ref.shape[0]
    keys = jnp.concatenate([first_ref[0], kept_ref[0], swapped_ref[0]], axis=0)
    values = jnp.concatenate([first_ref[1], kept_ref[1], swapped_ref[1]], axis=0)
    total_keys = None
    total_values = None
    for block in range(rows // BLOCK):
        here = slice(block * BLOCK, (block + 1) * BLOCK)
        grad = grad_ref[here, :]
        product = (grad.astype(F32) * mixed_ref[here, :].astype(F32)).T
        inner = jnp.sum(product, axis=0, keepdims=True)
        inner_ref[0, :, here] = jnp.broadcast_to(inner, (8, BLOCK))
        grad_queries, grad_keys, grad_values = attend_back(
            query_ref[here, :], grad, keys, values, lse_ref[0, 0:1, here], inner
        )
        grad_query_ref[here, :] = grad_queries
        total_keys = grad_keys if total_keys is None else total_keys + grad_keys
        total_values = grad_values if total_values is None else total_values + grad_values
    total_keys = (total_keys * SCALE).astype(BF16)
    total_values = total_values.astype(BF16)
    start = 0
    for ref in (grad_first_ref, grad_kept_ref, grad_swapped_ref):
        count = ref.shape[1]
        ref[0] = total_keys[start : start + count]
        ref[1] = total_values[start : start + count]
        start += count


def far_backward(queries, far, mixed, grad_mixed, lse):
    rows, features = queries.shape
    heads = features // HEAD_DIM
    return pl.pallas_call(
        far_back_kernel,
        grid=(heads,),
        in_specs=[column(rows)]
        + [pair(part.shape[1]) for part in far]
        + [column(rows)] * 2
        + [row_stat(rows)],
        out_specs=[pair(part.shape[1]) for part in far] + [column(rows), row_stat(rows)],
        out_shape=[jax.ShapeDtypeStruct(part.shape, BF16) for part in far]
        + [
            jax.ShapeDtypeStruct((rows, features), F32),
            jax.ShapeDtypeStruct((heads, 8, rows), F32),
        ],
        compiler_params=params(),
        name="far_backward",
    )(queries, *far, mixed, grad_mixed, lse)


def near_back_kernel(
    local, query_ref, key_ref, value_ref, coarse_ref, grad_ref, lse_ref, inner_ref, far_query_ref,
    grad_query_ref, grad_key_ref, grad_value_ref,
):
    rows = query_ref.shape[0]
    blocks = rows // BLOCK
    own = [[None] * blocks, [None] * blocks]
    pooled = [[None] * (2 * blocks) for _ in range(2 * local)]
    for block in range(blocks):
        here = slice(block * BLOCK, (block + 1) * BLOCK)
        keys = local_list(key_ref, coarse_ref.at[0], block, local, rows)
        values = local_list(value_ref, coarse_ref.at[1], block, local, rows)
        grad_queries, grad_keys, grad_values = attend_back(
            query_ref[here, :], grad_ref[here, :], keys, values,
            lse_ref[0, 0:1, here], inner_ref[0, 0:1, here],
        )
        grad_query_ref[here, :] = ((grad_queries + far_query_ref[here, :]) * SCALE).astype(BF16)
        for index, value in enumerate((grad_keys * SCALE, grad_values)):
            own[index][block] = value[:BLOCK]
            for level in range(1, local):
                sibling = block >> (level - 1) ^ 1
                start = BLOCK + (level - 1) * POOLED
                piece = value[start : start + POOLED]
                held = pooled[2 * level + index][sibling]
                pooled[2 * level + index][sibling] = piece if held is None else held + piece
    matrix = widen_matrix(BLOCK, POOLED, 1)
    for index, ref in enumerate((grad_key_ref, grad_value_ref)):
        for level in range(local - 1, 0, -1):
            for half in range(blocks >> (level - 1)):
                wide = nn(matrix, pooled[2 * level + index][half].astype(BF16))
                if level == 1:
                    own[index][half] = own[index][half] + wide
                else:
                    below = pooled[2 * (level - 1) + index]
                    below[2 * half] = below[2 * half] + wide[:POOLED]
                    below[2 * half + 1] = below[2 * half + 1] + wide[POOLED:]
        for block in range(blocks):
            ref[block * BLOCK : (block + 1) * BLOCK, :] = own[index][block].astype(BF16)


def near_backward(queries, key_states, value_states, coarse, grad_mixed, lse, inner, far_query, local):
    rows, features = queries.shape
    return pl.pallas_call(
        functools.partial(near_back_kernel, local),
        grid=(features // HEAD_DIM,),
        in_specs=[column(rows)] * 3
        + [pair(coarse.shape[1]), column(rows), row_stat(rows), row_stat(rows), column(rows)],
        out_specs=[column(rows)] * 3,
        out_shape=[jax.ShapeDtypeStruct((rows, features), BF16)] * 3,
        compiler_params=params(),
        name="near_backward",
    )(queries, key_states, value_states, coarse, grad_mixed, lse, inner, far_query)


def finish_kernel(local, key_ref, value_ref, *refs):
    parts, (grad_key_ref, grad_value_ref) = refs[:-2], refs[-2:]
    rows = key_ref.shape[0]
    spread = widen_matrix(rows, POOLED, local)
    for index, (near, out) in enumerate(((key_ref, grad_key_ref), (value_ref, grad_value_ref))):
        held = None
        for part in parts[::-1]:
            value = part[index].astype(F32)
            if held is not None:
                value = value + nn(widen_matrix(value.shape[0], held.shape[0], 1), held.astype(BF16))
            held = value
        out[...] = (near[...].astype(F32) + nn(spread, held.astype(BF16))).astype(BF16)


def finish(grad_key, grad_value, parts, local):
    rows, features = grad_key.shape
    width = min(features, 256)
    near = pl.BlockSpec((rows, width), lambda j: (0, j))
    return pl.pallas_call(
        functools.partial(finish_kernel, local),
        grid=(features // width,),
        in_specs=[near] * 2
        + [pl.BlockSpec((2, part.shape[1], width), lambda j: (0, 0, j)) for part in parts],
        out_specs=[near] * 2,
        out_shape=[jax.ShapeDtypeStruct((rows, features), BF16)] * 2,
        compiler_params=params(),
        name="finish",
    )(grad_key, grad_value, *parts)


def gather_far(summary, pack, cross):
    first = from_partner(summary, 0)
    chunks = []
    start = 0
    for bit in range(1, cross):
        count = POOLED >> bit
        chunks.append(from_partner(pack[:, start : start + count], bit))
        start += count
    for bit in range(1, cross - 1):
        sizes = [chunk.shape[1] for chunk in chunks[bit:]]
        sent = jnp.concatenate(chunks[bit:], axis=1)
        arrived = from_partner(sent, bit)
        start = 0
        for index, size in enumerate(sizes):
            chunks[bit + index] = jnp.concatenate(
                [chunks[bit + index], arrived[:, start : start + size]], axis=1
            )
            start += size
    kept = jnp.concatenate(chunks, axis=1)
    return first, kept, from_partner(kept, 0)


def added(first, second):
    return (first.astype(F32) + second.astype(F32)).astype(BF16)


def scatter_far(grad_first, grad_kept, grad_swapped, cross):
    parts = [from_partner(grad_first, 0)]
    kept = added(grad_kept, from_partner(grad_swapped, 0))
    half = POOLED // 2
    chunks = [kept[:, index * half : (index + 1) * half] for index in range(cross - 1)]
    for bit in range(cross - 2, 0, -1):
        sizes = [chunk.shape[1] // 2 for chunk in chunks[bit:]]
        sent = jnp.concatenate([chunk[:, chunk.shape[1] // 2 :] for chunk in chunks[bit:]], axis=1)
        arrived = from_partner(sent, bit)
        start = 0
        for index, size in enumerate(sizes):
            chunks[bit + index] = added(
                chunks[bit + index][:, :size], arrived[:, start : start + size]
            )
            start += size
    for bit in range(1, cross):
        parts.append(from_partner(chunks[bit - 1], bit))
    return parts


def solution_body(queries, key_states, value_states, out_weight, cotangent):
    rows, features = queries.shape
    cross = lax.axis_size("seq").bit_length() - 1
    local = (rows // POOLED).bit_length() - 1
    groups = lax.axis_size("head")
    piece = lax.all_gather(cotangent, "head", axis=1, tiled=True)
    coarse, summary, pack = pool(key_states, value_states, local, cross)
    far = gather_far(summary, pack, cross)
    near, stat = near_forward(queries, key_states, value_states, coarse, local)
    mixed, lse = far_forward(queries, far, near, stat)
    partial_out = jnp.dot(mixed, out_weight, preferred_element_type=F32).astype(BF16)
    attended = lax.psum_scatter(partial_out, "head", scatter_dimension=1, tiled=True)
    grad_mixed = nt(piece, out_weight).astype(BF16)
    grad_weight = lax.psum(tn(mixed, piece).astype(BF16), "seq")
    *grad_far, far_query, inner = far_backward(queries, far, mixed, grad_mixed, lse)
    parts = scatter_far(*grad_far, cross)
    grad_queries, grad_key, grad_value = near_backward(
        queries, key_states, value_states, coarse, grad_mixed, lse, inner, far_query, local
    )
    grad_keys, grad_values = finish(grad_key, grad_value, parts, local)
    return attended, grad_queries, grad_keys, grad_values, grad_weight


def solution(mesh):
    split = P("seq", "head")
    return jax.shard_map(
        solution_body,
        mesh=mesh,
        in_specs=(split, split, split, P("head", None), split),
        out_specs=(split, split, split, split, P("head", None)),
        check_vma=False,
    )
```

```python
import functools

import jax
import jax.numpy as jnp
from jax import lax
from jax.experimental import pallas as pl
from jax.experimental.pallas import tpu as pltpu
from jax.sharding import PartitionSpec as P

HEAD_DIM = 128
BLOCK = 256
POOLED = 128
SCALE = HEAD_DIM ** -0.5
SCALE2 = SCALE * 1.4426950408889634
VMEM = 48 * 1024 * 1024
WIDE_VMEM = 60 * 1024 * 1024
F32 = jnp.float32
BF16 = jnp.bfloat16


def params(limit=VMEM):
    return pltpu.CompilerParams(vmem_limit_bytes=limit)


def cost(micros, like):
    scale = 0.05 * micros * like.shape[0] * like.shape[1] / (1 << 20)
    return pl.CostEstimate(
        flops=int(scale * 1.15e9), bytes_accessed=int(scale * 3.6e6), transcendentals=0
    )


def nn(a, b):
    return lax.dot_general(a, b, (((1,), (0,)), ((), ())), preferred_element_type=F32)


def nt(a, b):
    return lax.dot_general(a, b, (((1,), (1,)), ((), ())), preferred_element_type=F32)


def tn(a, b):
    return lax.dot_general(a, b, (((0,), (0,)), ((), ())), preferred_element_type=F32)


def widen_matrix(rows, columns, shift):
    row = lax.broadcasted_iota(jnp.int32, (rows, columns), 0)
    column = lax.broadcasted_iota(jnp.int32, (rows, columns), 1)
    return jnp.where((row >> shift) == column, 0.5 ** shift, 0.0).astype(BF16)


def added(first, second):
    return (first.astype(F32) + second.astype(F32)).astype(BF16)


def tie(value, *others):
    return lax.optimization_barrier((value, *others))[0] if others else value


def from_partner(block, bit):
    count = lax.axis_size("seq")
    return lax.ppermute(block, "seq", [(low, low ^ 1 << bit) for low in range(count)])


def column(rows, width):
    return pl.BlockSpec((rows, width), lambda h: (0, h))


def row(rows, width):
    return pl.BlockSpec((width, rows), lambda h: (h, 0))


def pair(rows, width):
    return pl.BlockSpec((2, rows, width), lambda h: (0, 0, h))


def stat(rows, heads):
    return pl.BlockSpec((heads, 8, rows), lambda h: (h, 0, 0))


def lanes_of(ref):
    return [slice(start, start + HEAD_DIM) for start in range(0, ref.shape[-1], HEAD_DIM)]


def blocks_of(ref):
    return [slice(start, start + BLOCK) for start in range(0, ref.shape[0], BLOCK)]


def step_heads(features):
    return min(features // HEAD_DIM, 2)


def pool_kernel(local, cross, key_ref, value_ref, coarse_ref, *refs):
    pooled, held_ref = refs[:-1], refs[-1]
    for index, ref in enumerate((key_ref, value_ref)):
        for head, lanes in enumerate(lanes_of(ref)):
            held = held_ref.at[index, head]
            count = ref.shape[0]
            coarse_start = 0
            held[...] = ref[:, lanes].astype(F32)
            for level in range(1, local + cross):
                count //= 2
                even = held[pl.ds(0, count, stride=2), :]
                odd = held[pl.ds(1, count, stride=2), :]
                rows = (0.5 * (even + odd)).astype(BF16)
                if level < local:
                    coarse_ref[index, coarse_start : coarse_start + count, lanes] = rows
                    coarse_start += count
                else:
                    pooled[level - local][index, :, lanes] = rows
                held[0:count, :] = rows.astype(F32)


def pool(key_states, value_states, local, cross):
    rows, features = key_states.shape
    heads = step_heads(features)
    width = heads * HEAD_DIM
    counts = [sum(rows >> level for level in range(1, local))]
    counts += [POOLED >> bit for bit in range(cross)]
    return pl.pallas_call(
        functools.partial(pool_kernel, local, cross),
        grid=(features // width,),
        in_specs=[column(rows, width)] * 2,
        out_specs=[pair(count, width) for count in counts],
        out_shape=[jax.ShapeDtypeStruct((2, count, features), BF16) for count in counts],
        scratch_shapes=[pltpu.VMEM((2, heads, rows, HEAD_DIM), F32)],
        compiler_params=params(WIDE_VMEM),
        cost_estimate=cost(5, key_states),
        name="pool",
    )(key_states, value_states)


def local_starts(block, local, rows):
    starts = []
    offset = 0
    for level in range(1, local):
        starts.append(offset + (block >> (level - 1) ^ 1) * POOLED)
        offset += rows >> level
    return starts


def local_list(own, coarse, block, local):
    parts = [own[block * BLOCK : (block + 1) * BLOCK]]
    parts += [coarse[at : at + POOLED] for at in local_starts(block, local, own.shape[0])]
    return jnp.concatenate(parts, axis=0)


def lane_max(scores):
    count = scores.shape[1]
    while count > HEAD_DIM:
        half = (count // HEAD_DIM + 1) // 2 * HEAD_DIM
        top = jnp.maximum(scores[:, : count - half], scores[:, half:])
        if 2 * half > count:
            top = jnp.concatenate([top, scores[:, count - half : half]], axis=1)
        scores, count = top, half
    return jnp.max(scores, axis=1, keepdims=True)


def attend(queries, keys, values):
    scores = nt(queries, keys)
    top = lane_max(scores)
    weights = jnp.exp2((scores - top) * SCALE2).astype(BF16)
    ones = jnp.ones((values.shape[0], HEAD_DIM), BF16)
    mixed = nn(weights, jnp.concatenate([values, ones], axis=1))
    total = mixed[:, HEAD_DIM:]
    return mixed[:, :HEAD_DIM] / total, top * SCALE2 + jnp.log2(total)


def near_kernel(local, query_ref, key_ref, value_ref, coarse_ref, out_ref, lse_ref):
    for head, lanes in enumerate(lanes_of(query_ref)):
        keys, values = key_ref[:, lanes], value_ref[:, lanes]
        coarse_keys, coarse_values = coarse_ref[0, :, lanes], coarse_ref[1, :, lanes]
        for block, here in enumerate(blocks_of(query_ref)):
            mixed, lse = attend(
                query_ref[here, lanes],
                local_list(keys, coarse_keys, block, local),
                local_list(values, coarse_values, block, local),
            )
            out_ref[here, lanes] = mixed.astype(BF16)
            lse_ref[head, :, here] = lse.T[:8]


def far_kernel(parts, query_ref, *refs):
    far, (near_ref, near_lse_ref, mixed_ref, lse_ref) = refs[:parts], refs[parts:]
    for head, lanes in enumerate(lanes_of(query_ref)):
        keys = jnp.concatenate([part[0, :, lanes] for part in far], axis=0)
        values = jnp.concatenate([part[1, :, lanes] for part in far], axis=0)
        for here in blocks_of(query_ref):
            mixed, lse = attend(query_ref[here, lanes], keys, values)
            near_lse = jnp.broadcast_to(near_lse_ref[head, 0:1, here], (HEAD_DIM, BLOCK)).T
            top = jnp.maximum(near_lse, lse)
            near_share = jnp.exp2(near_lse - top)
            far_share = jnp.exp2(lse - top)
            total = near_share + far_share
            both = near_ref[here, lanes].astype(F32) * near_share + mixed * far_share
            mixed_ref[here, lanes] = (both / total).astype(BF16)
            lse_ref[head, :, here] = (top + jnp.log2(total)).T[:8]


def near_forward(queries, key_states, value_states, coarse, local):
    rows, features = queries.shape
    heads = step_heads(features)
    width = heads * HEAD_DIM
    return pl.pallas_call(
        functools.partial(near_kernel, local),
        grid=(features // width,),
        in_specs=[column(rows, width)] * 3 + [pair(coarse.shape[1], width)],
        out_specs=[column(rows, width), stat(rows, heads)],
        out_shape=[
            jax.ShapeDtypeStruct((rows, features), BF16),
            jax.ShapeDtypeStruct((features // HEAD_DIM, 8, rows), F32),
        ],
        compiler_params=params(),
        cost_estimate=cost(9, queries),
        name="near_forward",
    )(queries, key_states, value_states, coarse)


def far_forward(queries, far, near, near_lse):
    rows, features = queries.shape
    heads = step_heads(features)
    width = heads * HEAD_DIM
    return pl.pallas_call(
        functools.partial(far_kernel, len(far)),
        grid=(features // width,),
        in_specs=[column(rows, width)]
        + [pair(part.shape[1], width) for part in far]
        + [column(rows, width), stat(rows, heads)],
        out_specs=[column(rows, width), stat(rows, heads)],
        out_shape=[
            jax.ShapeDtypeStruct((rows, features), BF16),
            jax.ShapeDtypeStruct((features // HEAD_DIM, 8, rows), F32),
        ],
        compiler_params=params(WIDE_VMEM),
        cost_estimate=cost(10, queries),
        name="far_forward",
    )(queries, *far, near, near_lse)


def attend_back(queries, grad_mixed, keys, values, keys_across, lse, inner):
    weights = jnp.exp2(nt(keys, queries) * SCALE2 - lse)
    grad_probs = nt(values, grad_mixed)
    grad_scores = (weights * (grad_probs - inner)).astype(BF16)
    both = jnp.concatenate([grad_mixed, queries], axis=1)
    grad_values = nn(weights.astype(BF16), both)[:, :HEAD_DIM]
    grad_keys = nn(grad_scores, both)[:, HEAD_DIM:]
    return nn(keys_across, grad_scores), grad_keys, grad_values


def far_back_kernel(parts, query_ref, mixed_ref, grad_ref, lse_ref, *refs):
    far, grad_far = refs[:parts], refs[parts : 2 * parts]
    grad_query_ref, inner_ref = refs[2 * parts :]
    for head, lanes in enumerate(lanes_of(query_ref)):
        keys = jnp.concatenate([part[0, :, lanes] for part in far], axis=0)
        values = jnp.concatenate([part[1, :, lanes] for part in far], axis=0)
        keys_across = keys.T
        total_keys = total_values = None
        for here in blocks_of(query_ref):
            grad = grad_ref[here, lanes]
            product = (grad.astype(F32) * mixed_ref[here, lanes].astype(F32)).T
            inner = jnp.sum(product, axis=0, keepdims=True)
            inner_ref[head, :, here] = jnp.broadcast_to(inner, (8, BLOCK))
            grad_queries, grad_keys, grad_values = attend_back(
                query_ref[here, lanes], grad, keys, values, keys_across,
                lse_ref[head, 0:1, here], inner,
            )
            grad_query_ref[lanes, here] = grad_queries.astype(BF16)
            total_keys = grad_keys if total_keys is None else total_keys + grad_keys
            total_values = grad_values if total_values is None else total_values + grad_values
        total_keys = (total_keys * SCALE).astype(BF16)
        total_values = total_values.astype(BF16)
        start = 0
        for ref in grad_far:
            count = ref.shape[1]
            ref[0, :, lanes] = total_keys[start : start + count]
            ref[1, :, lanes] = total_values[start : start + count]
            start += count


def far_backward(queries, far, mixed, grad_mixed, lse):
    rows, features = queries.shape
    heads = step_heads(features)
    width = heads * HEAD_DIM
    far_specs = [pair(part.shape[1], width) for part in far]
    return pl.pallas_call(
        functools.partial(far_back_kernel, len(far)),
        grid=(features // width,),
        in_specs=[column(rows, width)] * 3 + [stat(rows, heads)] + far_specs,
        out_specs=far_specs + [row(rows, width), stat(rows, heads)],
        out_shape=[jax.ShapeDtypeStruct(part.shape, BF16) for part in far]
        + [
            jax.ShapeDtypeStruct((features, rows), BF16),
            jax.ShapeDtypeStruct((features // HEAD_DIM, 8, rows), F32),
        ],
        compiler_params=params(WIDE_VMEM),
        cost_estimate=cost(14, queries),
        name="far_backward",
    )(queries, mixed, grad_mixed, lse, *far)


def near_back_kernel(
    local, parts, query_ref, key_ref, value_ref, coarse_ref, grad_ref, lse_ref, inner_ref,
    far_query_ref, *refs,
):
    far, (grad_query_ref, grad_key_ref, grad_value_ref) = refs[:parts], refs[-3:]
    rows = query_ref.shape[0]
    blocks = rows // BLOCK
    matrix = widen_matrix(BLOCK, POOLED, 1)
    for head, lanes in enumerate(lanes_of(query_ref)):
        keys, values = key_ref[:, lanes], value_ref[:, lanes]
        coarse_keys, coarse_values = coarse_ref[0, :, lanes], coarse_ref[1, :, lanes]
        keys_across, coarse_across = keys.T, coarse_keys.T
        own = [[None] * blocks, [None] * blocks]
        pooled = [[[None] * (blocks >> (level - 1)) for level in range(1, local)] for _ in range(2)]
        for index in range(2):
            held = None
            for part in far[::-1]:
                value = part[index, :, lanes].astype(F32)
                if held is not None:
                    wider = widen_matrix(value.shape[0], held.shape[0], 1)
                    value = value + nn(wider, held.astype(BF16))
                held = value
            pooled[index].append([held])
        for block, here in enumerate(blocks_of(query_ref)):
            starts = local_starts(block, local, rows)
            across = [keys_across[:, here]] + [coarse_across[:, at : at + POOLED] for at in starts]
            grad_queries, grad_keys, grad_values = attend_back(
                query_ref[here, lanes], grad_ref[here, lanes],
                local_list(keys, coarse_keys, block, local),
                local_list(values, coarse_values, block, local),
                jnp.concatenate(across, axis=1),
                lse_ref[head, 0:1, here], inner_ref[head, 0:1, here],
            )
            grad_queries = (grad_queries + far_query_ref[lanes, here].astype(F32)) * SCALE
            grad_query_ref[here, lanes] = grad_queries.T.astype(BF16)
            for index, value in enumerate((grad_keys * SCALE, grad_values)):
                own[index][block] = value[:BLOCK]
                for level in range(1, local):
                    sibling = block >> (level - 1) ^ 1
                    start = BLOCK + (level - 1) * POOLED
                    piece = value[start : start + POOLED]
                    held = pooled[index][level - 1]
                    held[sibling] = piece if held[sibling] is None else held[sibling] + piece
        for index, ref in enumerate((grad_key_ref, grad_value_ref)):
            for level in range(local, 0, -1):
                for half in range(len(pooled[index][level - 1])):
                    wide = nn(matrix, pooled[index][level - 1][half].astype(BF16))
                    if level == 1:
                        own[index][half] = own[index][half] + wide
                    else:
                        below = pooled[index][level - 2]
                        below[2 * half] = below[2 * half] + wide[:POOLED]
                        below[2 * half + 1] = below[2 * half + 1] + wide[POOLED:]
            for block, here in enumerate(blocks_of(query_ref)):
                ref[here, lanes] = own[index][block].astype(BF16)


def near_backward(operands, grads, local, part, parts):
    queries, coarse, pooled = operands[0], operands[3], operands[8:]
    rows, features = queries.shape
    heads = step_heads(features)
    width = heads * HEAD_DIM
    steps = features // width // parts
    first = part * steps

    def wide(count):
        return pl.BlockSpec((count, width), lambda h: (0, first + h))

    def pair_at(count):
        return pl.BlockSpec((2, count, width), lambda h: (0, 0, first + h))

    stats = pl.BlockSpec((heads, 8, rows), lambda h: (first + h, 0, 0))
    across = pl.BlockSpec((width, rows), lambda h: (first + h, 0))
    count = len(operands)
    return pl.pallas_call(
        functools.partial(near_back_kernel, local, len(pooled)),
        grid=(steps,),
        in_specs=[wide(rows)] * 3
        + [pair_at(coarse.shape[1]), wide(rows), stats, stats, across]
        + [pair_at(rows_of.shape[1]) for rows_of in pooled]
        + [pl.BlockSpec(memory_space=pl.ANY)] * len(grads),
        out_specs=[wide(rows)] * 3,
        out_shape=[jax.ShapeDtypeStruct((rows, features), BF16)] * 3,
        input_output_aliases={count + index: index for index in range(len(grads))},
        compiler_params=params(),
        cost_estimate=cost(18 / parts, queries),
        name="near_backward",
    )(*operands, *grads)


def index_call(
    kernel, name, micros, scalars, grid, in_specs, out_spec, out_shape, args, limit=VMEM, aliases={}
):
    return pl.pallas_call(
        kernel,
        grid_spec=pltpu.PrefetchScalarGridSpec(
            num_scalar_prefetch=1, grid=grid, in_specs=in_specs, out_specs=out_spec
        ),
        out_shape=out_shape,
        compiler_params=params(limit),
        input_output_aliases=aliases,
        cost_estimate=cost(micros, args[0]),
        name=name,
    )(scalars, *args)


def project_kernel(which_ref, mixed_ref, weight_ref, *refs):
    share = nn(mixed_ref[...], weight_ref[...]).astype(BF16)
    if len(refs) == 2:
        share = (share.astype(F32) + refs[0][...].astype(F32)).astype(BF16)
    refs[-1][...] = share


def project(mixed, out_weight, which, arrived=None):
    rows, features = mixed.shape
    width = min(512, features)
    steps = features // width
    out = pl.BlockSpec((rows, width), lambda j, which: (0, j))
    return index_call(
        project_kernel, "project", 5, which, (steps,),
        [
            pl.BlockSpec((rows, features), lambda j, which: (0, 0)),
            pl.BlockSpec((features, width), lambda j, which: (0, which[0] * steps + j)),
        ]
        + ([] if arrived is None else [out]),
        out, jax.ShapeDtypeStruct((rows, features), BF16),
        (mixed, out_weight) if arrived is None else (mixed, out_weight, arrived),
    )


def mix_back_kernel(which_ref, own_ref, other_ref, own_weight_ref, other_weight_ref, out_ref):
    total = nt(own_ref[...], own_weight_ref[...]) + nt(other_ref[...], other_weight_ref[...])
    out_ref[...] = total.astype(BF16)


def mix_back(own, other, out_weight, which):
    rows, features = own.shape
    width = min(512, features)
    whole = pl.BlockSpec((rows, features), lambda j, which: (0, 0))
    return index_call(
        mix_back_kernel, "mix_back", 8, which, (features // width,),
        [
            whole,
            whole,
            pl.BlockSpec((width, features), lambda j, which: (j, which[0])),
            pl.BlockSpec((width, features), lambda j, which: (j, 1 - which[0])),
        ],
        pl.BlockSpec((rows, width), lambda j, which: (0, j)),
        jax.ShapeDtypeStruct((rows, features), BF16),
        (own, other, out_weight, out_weight),
    )


def weight_kernel(which_ref, mixed_ref, grad_ref, mine_ref, sent_ref):
    share = tn(mixed_ref[...], grad_ref[...]).astype(BF16)

    @pl.when(pl.program_id(0) == 0)
    def first():
        sent_ref[...] = share

    @pl.when(pl.program_id(0) == 1)
    def second():
        mine_ref[...] = share


def weight_halves(mixed, grad, which):
    rows, features = mixed.shape
    half = features // 2
    columns = grad.shape[1]
    steps = max(columns // 512, 1)
    width = columns // steps

    def mine_index(i, j, which):
        return 0, jnp.where(i == 1, j, 0)

    def sent_index(i, j, which):
        return 0, jnp.where(i == 0, j, steps - 1)

    return index_call(
        weight_kernel, "weight_halves", 4, which[None], (2, steps),
        [
            pl.BlockSpec((rows, half), lambda i, j, which: (0, 1 - i ^ which[0])),
            pl.BlockSpec((rows, width), lambda i, j, which: (0, j)),
        ],
        [pl.BlockSpec((half, width), mine_index), pl.BlockSpec((half, width), sent_index)],
        [jax.ShapeDtypeStruct((half, columns), BF16)] * 2, (mixed, grad),
    )


def add_kernel(which_ref, first_ref, second_ref, mine_ref, sent_ref):
    total = added(first_ref[...], second_ref[...])

    @pl.when(pl.program_id(0) == 0)
    def first():
        sent_ref[...] = total

    @pl.when(pl.program_id(0) == 1)
    def second():
        mine_ref[...] = total


def add_halves(first, second, which, micros):
    rows, columns = first.shape
    half = rows // 2
    spec = pl.BlockSpec((half, columns), lambda j, which: (1 - j ^ which[0], 0))
    out = pl.BlockSpec((half, columns), lambda j, which: (0, 0))
    return index_call(
        add_kernel, "add_halves", micros, which[None], (2,), [spec, spec], [out, out],
        [jax.ShapeDtypeStruct((half, columns), BF16)] * 2, (first, second), limit=WIDE_VMEM,
    )


def place_kernel(chunks, where_ref, first_ref, second_ref, *refs):
    out_ref = refs[-1]
    for index, ref in enumerate((first_ref, second_ref)):

        @pl.when(pl.program_id(0) == index)
        def copy(index=index, ref=ref):
            size = ref.shape[0] // chunks
            for chunk in range(chunks):
                start = pl.multiple_of((chunk ^ where_ref[index]) * size, size)
                out_ref[pl.ds(start, size), :] = ref[chunk * size : (chunk + 1) * size, :]


def place(first, second, chunks, where, held=None):
    half, columns = first.shape
    spec = pl.BlockSpec((half, columns), lambda step, where: (0, 0))
    return index_call(
        functools.partial(place_kernel, chunks), "place", 2, where, (2,),
        [spec, spec] + ([] if held is None else [pl.BlockSpec(memory_space=pl.ANY)]),
        pl.BlockSpec((half, columns), lambda step, where: (where[2], step ^ where[3])),
        jax.ShapeDtypeStruct((2 * half, 2 * columns), BF16),
        (first, second) if held is None else (first, second, held),
        aliases={} if held is None else {3: 0},
    )


def gather_far(pooled, meanwhile):
    cross = len(pooled)
    first, *chunks = [from_partner(rows, bit) for bit, rows in enumerate(pooled)]
    for bit in range(1, cross - 1):
        sizes = [chunk.shape[1] for chunk in chunks[bit:]]
        sent = jnp.concatenate(chunks[bit:], axis=1)
        if bit == 1:
            sent = tie(sent, meanwhile)
        arrived = from_partner(sent, bit)
        start = 0
        for index, size in enumerate(sizes):
            chunks[bit + index] = jnp.concatenate(
                [chunks[bit + index], arrived[:, start : start + size]], axis=1
            )
            start += size
    kept = jnp.concatenate(chunks, axis=1)
    return first, kept, from_partner(kept, 0)


def scatter_far(grad_first, grad_kept, grad_swapped, cross):
    parts = [from_partner(grad_first, 0)]
    arrived, after = yield move(grad_swapped, 0)
    kept = added(tie(grad_kept, *after), arrived)
    half = POOLED // 2
    chunks = [kept[:, index * half : (index + 1) * half] for index in range(cross - 1)]
    for bit in range(cross - 2, 0, -1):
        sizes = [chunk.shape[1] // 2 for chunk in chunks[bit:]]
        sent = jnp.concatenate([chunk[:, chunk.shape[1] // 2 :] for chunk in chunks[bit:]], axis=1)
        arrived, after = yield move(sent, bit, chunks[-1])
        chunks = list(tie(tuple(chunks), *after))
        start = 0
        for index, size in enumerate(sizes):
            chunks[bit + index] = added(
                chunks[bit + index][:, :size], arrived[:, start : start + size]
            )
            start += size
    parts += [from_partner(chunk, bit + 1) for bit, chunk in enumerate(chunks)]
    yield chunks[-1], tuple(parts)


def move(rows, bit, kept=None):
    return rows if kept is None else kept, from_partner(rows, bit)


def seq_bit(bit):
    return lax.axis_index("seq") >> bit & 1


def sum_rows(mine, sent, bits, micros):
    arrived, after = yield move(sent, 0, mine)
    for bit in bits[:-1]:
        mine, sent = add_halves(tie(mine, *after), arrived, seq_bit(bit), micros if after else 1)
        arrived, after = yield move(sent, bit, mine)
    rows = added(tie(mine, *after), arrived)
    arrived, after = yield move(rows, bits[-1])
    rows = added(tie(rows, *after), arrived)
    for bit in bits[-2::-1]:
        arrived, after = yield move(rows, bit)
        rows = jnp.concatenate([tie(rows, *after), arrived], axis=0)
    yield rows, move(rows, 0)


class Chain:
    def __init__(self, steps, count):
        self.steps, self.left = steps, count
        self.kept, self.moving = next(steps)

    def advance(self, *after):
        self.left -= 1
        self.kept, self.moving = self.steps.send((self.moving, after))


def chunk_index(bits):
    index = 0
    for bit in bits[:-1]:
        index = index * 2 + seq_bit(bit)
    return index


def solution_body(queries, key_states, value_states, out_weight, cotangent):
    rows, features = queries.shape
    cross = lax.axis_size("seq").bit_length() - 1
    local = (rows // POOLED).bit_length() - 1
    groups = lax.axis_size("head")
    group = lax.axis_index("head")
    swap = [(0, 1), (1, 0)]
    if groups == 2:
        other = lax.ppermute(cotangent, "head", swap)
    else:
        piece = lax.all_gather(cotangent, "head", axis=1, tiled=True)
    coarse, *pooled = pool(key_states, value_states, local, cross)
    near, near_lse = near_forward(queries, key_states, value_states, coarse, local)
    far = gather_far(pooled, near)
    mixed, lse = far_forward(queries, far, near, near_lse)
    if groups == 2:
        share = project(mixed, out_weight, (1 - group)[None])
        shared = lax.ppermute(share, "head", swap)
        first, second, flip = tie(cotangent, share), other, group
    else:
        partial_out = jnp.dot(mixed, out_weight, preferred_element_type=F32).astype(BF16)
        attended = lax.psum_scatter(partial_out, "head", scatter_dimension=1, tiled=True)
        grad_mixed = nt(piece, out_weight).astype(BF16)
        middle = piece.shape[1] // 2
        first, second, flip = piece[:, :middle], piece[:, middle:], 0
    first_bits = list(range(1, cross))
    second_bits = first_bits[1:] + first_bits[:1]
    first_halves = weight_halves(mixed, first, seq_bit(0))
    first_sum = Chain(sum_rows(*first_halves, first_bits, 1), 2 * cross - 2)
    second_halves = weight_halves(mixed, tie(second, *first_halves), seq_bit(0))
    second_sum = Chain(sum_rows(*second_halves, second_bits, 400), 2 * cross - 2)
    first_sum.advance()
    second_sum.advance()
    if groups == 2:
        ready = tie(cotangent, first_sum.kept, second_sum.kept)
        grad_mixed = mix_back(ready, other, out_weight, group[None])
    *grad_far, far_query, inner = far_backward(queries, far, mixed, grad_mixed, lse)
    far_sum = Chain(scatter_far(*grad_far, cross), cross - 1)
    arrivals = (inner, shared) if groups == 2 else (inner,)
    first_sum.advance(*arrivals)
    second_sum.advance(*arrivals)
    far_sum.advance(first_sum.kept, second_sum.kept)
    if groups == 2:
        attended = project(tie(mixed, far_sum.kept), out_weight, group[None], shared)
    far_sum.advance(*([attended] if groups == 2 else []))
    first_sum.advance(far_sum.kept)
    while far_sum.left:
        far_sum.advance(first_sum.kept)
    second_sum.advance(far_sum.kept)
    first_sum.advance(second_sum.kept, *far_sum.moving)
    second_sum.advance(*far_sum.moving)
    inner = tie(inner, first_sum.kept, second_sum.kept)
    operands = (
        queries, key_states, value_states, coarse, grad_mixed, lse, inner, far_query,
        *far_sum.moving,
    )
    parts = 2 if features % (4 * HEAD_DIM) == 0 else 1
    grads = ()
    for part in range(parts):
        grads = near_backward(operands, grads, local, part, parts)
        if first_sum.left:
            first_sum.advance(grads[0])
            second_sum.advance(grads[0])
    grad_queries, grad_keys, grad_values = grads
    for chain in (first_sum, second_sum):
        while chain.left:
            chain.advance()
    spots = [chunk_index(first_bits), chunk_index(second_bits)]
    flip = jnp.asarray(flip, jnp.int32)
    chunks = 1 << (cross - 2)
    (first_mine, first_other), (second_mine, second_other) = first_sum.moving, second_sum.moving
    grad_weight = place(
        first_mine, second_mine, chunks, jnp.stack([*spots, seq_bit(0), flip])
    )
    grad_weight = place(
        first_other, second_other, chunks, jnp.stack([*spots, 1 - seq_bit(0), flip]), grad_weight
    )
    return attended, grad_queries, grad_keys, grad_values, grad_weight


def solution(mesh):
    split = P("seq", "head")
    return jax.shard_map(
        solution_body,
        mesh=mesh,
        in_specs=(split, split, split, P("head", None), split),
        out_specs=(split, split, split, split, P("head", None)),
        check_vma=False,
    )
```

```python
import functools

import jax
import jax.numpy as jnp
from jax import lax
from jax.experimental import pallas as pl
from jax.experimental.pallas import tpu as pltpu
from jax.sharding import PartitionSpec as P

HEAD_DIM = 128
BLOCK = 256
POOLED = 128
SCALE = HEAD_DIM ** -0.5
SCALE2 = SCALE * 1.4426950408889634
VMEM = 48 * 1024 * 1024
WIDE_VMEM = 60 * 1024 * 1024
F32 = jnp.float32
BF16 = jnp.bfloat16


def params(limit=VMEM):
    return pltpu.CompilerParams(vmem_limit_bytes=limit)


def cost(micros, like):
    scale = 0.05 * micros * like.shape[0] * like.shape[1] / (1 << 20)
    return pl.CostEstimate(
        flops=int(scale * 1.15e9), bytes_accessed=int(scale * 3.6e6), transcendentals=0
    )


def nn(a, b):
    return lax.dot_general(a, b, (((1,), (0,)), ((), ())), preferred_element_type=F32)


def nt(a, b):
    return lax.dot_general(a, b, (((1,), (1,)), ((), ())), preferred_element_type=F32)


def tn(a, b):
    return lax.dot_general(a, b, (((0,), (0,)), ((), ())), preferred_element_type=F32)


def widen_matrix(rows, columns, shift):
    row = lax.broadcasted_iota(jnp.int32, (rows, columns), 0)
    column = lax.broadcasted_iota(jnp.int32, (rows, columns), 1)
    return jnp.where((row >> shift) == column, 0.5 ** shift, 0.0).astype(BF16)


def added(first, second):
    return (first.astype(F32) + second.astype(F32)).astype(BF16)


def tie(value, *others):
    return lax.optimization_barrier((value, *others))[0] if others else value


def from_partner(block, bit):
    count = lax.axis_size("seq")
    return lax.ppermute(block, "seq", [(low, low ^ 1 << bit) for low in range(count)])


def column(rows, width):
    return pl.BlockSpec((rows, width), lambda h: (0, h))


def row(rows, width):
    return pl.BlockSpec((width, rows), lambda h: (h, 0))


def pair(rows, width):
    return pl.BlockSpec((2, rows, width), lambda h: (0, 0, h))


def stat(rows, heads):
    return pl.BlockSpec((heads, 8, rows), lambda h: (h, 0, 0))


def lanes_of(ref):
    return [slice(start, start + HEAD_DIM) for start in range(0, ref.shape[-1], HEAD_DIM)]


def blocks_of(ref):
    return [slice(start, start + BLOCK) for start in range(0, ref.shape[0], BLOCK)]


def step_heads(features, most=2):
    return min(features // HEAD_DIM, most)


def pool_kernel(local, cross, key_ref, value_ref, coarse_ref, *refs):
    pooled, held_ref = refs[:-1], refs[-1]
    for index, ref in enumerate((key_ref, value_ref)):
        for head, lanes in enumerate(lanes_of(ref)):
            held = held_ref.at[index, head]
            count = ref.shape[0]
            coarse_start = 0
            held[...] = ref[:, lanes].astype(F32)
            for level in range(1, local + cross):
                count //= 2
                even = held[pl.ds(0, count, stride=2), :]
                odd = held[pl.ds(1, count, stride=2), :]
                rows = (0.5 * (even + odd)).astype(BF16)
                if level < local:
                    coarse_ref[index, coarse_start : coarse_start + count, lanes] = rows
                    coarse_start += count
                else:
                    pooled[level - local][index, :, lanes] = rows
                held[0:count, :] = rows.astype(F32)


def pool(key_states, value_states, local, cross):
    rows, features = key_states.shape
    heads = step_heads(features)
    width = heads * HEAD_DIM
    counts = [sum(rows >> level for level in range(1, local))]
    counts += [POOLED >> bit for bit in range(cross)]
    return pl.pallas_call(
        functools.partial(pool_kernel, local, cross),
        grid=(features // width,),
        in_specs=[column(rows, width)] * 2,
        out_specs=[pair(count, width) for count in counts],
        out_shape=[jax.ShapeDtypeStruct((2, count, features), BF16) for count in counts],
        scratch_shapes=[pltpu.VMEM((2, heads, rows, HEAD_DIM), F32)],
        compiler_params=params(WIDE_VMEM),
        cost_estimate=cost(5, key_states),
        name="pool",
    )(key_states, value_states)


def local_starts(block, local, rows):
    starts = []
    offset = 0
    for level in range(1, local):
        starts.append(offset + (block >> (level - 1) ^ 1) * POOLED)
        offset += rows >> level
    return starts


def local_list(own, coarse, block, local):
    parts = [own[block * BLOCK : (block + 1) * BLOCK]]
    parts += [coarse[at : at + POOLED] for at in local_starts(block, local, own.shape[0])]
    return jnp.concatenate(parts, axis=0)


def lane_max(scores):
    count = scores.shape[1]
    while count > HEAD_DIM:
        half = (count // HEAD_DIM + 1) // 2 * HEAD_DIM
        top = jnp.maximum(scores[:, : count - half], scores[:, half:])
        if 2 * half > count:
            top = jnp.concatenate([top, scores[:, count - half : half]], axis=1)
        scores, count = top, half
    return jnp.max(scores, axis=1, keepdims=True)


def attend(queries, keys, values):
    scores = nt(queries, keys)
    top = lane_max(scores)
    weights = jnp.exp2((scores - top) * SCALE2).astype(BF16)
    ones = jnp.ones((values.shape[0], HEAD_DIM), BF16)
    mixed = nn(weights, jnp.concatenate([values, ones], axis=1))
    total = mixed[:, HEAD_DIM:]
    return mixed[:, :HEAD_DIM] / total, top * SCALE2 + jnp.log2(total)


def near_kernel(local, query_ref, key_ref, value_ref, coarse_ref, out_ref, lse_ref):
    for head, lanes in enumerate(lanes_of(query_ref)):
        keys, values = key_ref[:, lanes], value_ref[:, lanes]
        coarse_keys, coarse_values = coarse_ref[0, :, lanes], coarse_ref[1, :, lanes]
        for block, here in enumerate(blocks_of(query_ref)):
            mixed, lse = attend(
                query_ref[here, lanes],
                local_list(keys, coarse_keys, block, local),
                local_list(values, coarse_values, block, local),
            )
            out_ref[here, lanes] = mixed.astype(BF16)
            lse_ref[head, :, here] = lse.T[:8]


def far_kernel(parts, query_ref, *refs):
    far, (near_ref, near_lse_ref, mixed_ref, lse_ref) = refs[:parts], refs[parts:]
    for head, lanes in enumerate(lanes_of(query_ref)):
        keys = jnp.concatenate([part[0, :, lanes] for part in far], axis=0)
        values = jnp.concatenate([part[1, :, lanes] for part in far], axis=0)
        for here in blocks_of(query_ref):
            mixed, lse = attend(query_ref[here, lanes], keys, values)
            near_lse = jnp.broadcast_to(near_lse_ref[head, 0:1, here], (HEAD_DIM, BLOCK)).T
            top = jnp.maximum(near_lse, lse)
            near_share = jnp.exp2(near_lse - top)
            far_share = jnp.exp2(lse - top)
            total = near_share + far_share
            both = near_ref[here, lanes].astype(F32) * near_share + mixed * far_share
            mixed_ref[here, lanes] = (both / total).astype(BF16)
            lse_ref[head, :, here] = (top + jnp.log2(total)).T[:8]


def near_forward(queries, key_states, value_states, coarse, local):
    rows, features = queries.shape
    heads = step_heads(features, 4)
    width = heads * HEAD_DIM
    return pl.pallas_call(
        functools.partial(near_kernel, local),
        grid=(features // width,),
        in_specs=[column(rows, width)] * 3 + [pair(coarse.shape[1], width)],
        out_specs=[column(rows, width), stat(rows, heads)],
        out_shape=[
            jax.ShapeDtypeStruct((rows, features), BF16),
            jax.ShapeDtypeStruct((features // HEAD_DIM, 8, rows), F32),
        ],
        compiler_params=params(),
        cost_estimate=cost(9, queries),
        name="near_forward",
    )(queries, key_states, value_states, coarse)


def far_forward(queries, far, near, near_lse):
    rows, features = queries.shape
    heads = step_heads(features)
    width = heads * HEAD_DIM
    return pl.pallas_call(
        functools.partial(far_kernel, len(far)),
        grid=(features // width,),
        in_specs=[column(rows, width)]
        + [pair(part.shape[1], width) for part in far]
        + [column(rows, width), stat(rows, heads)],
        out_specs=[column(rows, width), stat(rows, heads)],
        out_shape=[
            jax.ShapeDtypeStruct((rows, features), BF16),
            jax.ShapeDtypeStruct((features // HEAD_DIM, 8, rows), F32),
        ],
        compiler_params=params(WIDE_VMEM),
        cost_estimate=cost(10, queries),
        name="far_forward",
    )(queries, *far, near, near_lse)


def attend_back(queries, grad_mixed, keys, values, keys_across, lse, inner):
    weights = jnp.exp2(nt(keys, queries) * SCALE2 - lse)
    grad_probs = nt(values, grad_mixed)
    grad_scores = (weights * (grad_probs - inner)).astype(BF16)
    both = jnp.concatenate([grad_mixed, queries], axis=1)
    grad_values = nn(weights.astype(BF16), both)[:, :HEAD_DIM]
    grad_keys = nn(grad_scores, both)[:, HEAD_DIM:]
    return nn(keys_across, grad_scores), grad_keys, grad_values


def far_back_kernel(parts, query_ref, mixed_ref, grad_ref, lse_ref, *refs):
    far, grad_far = refs[:parts], refs[parts : 2 * parts]
    grad_query_ref, inner_ref = refs[2 * parts :]
    for head, lanes in enumerate(lanes_of(query_ref)):
        keys = jnp.concatenate([part[0, :, lanes] for part in far], axis=0)
        values = jnp.concatenate([part[1, :, lanes] for part in far], axis=0)
        keys_across = keys.T
        total_keys = total_values = None
        for here in blocks_of(query_ref):
            grad = grad_ref[here, lanes]
            product = (grad.astype(F32) * mixed_ref[here, lanes].astype(F32)).T
            inner = jnp.sum(product, axis=0, keepdims=True)
            inner_ref[head, :, here] = jnp.broadcast_to(inner, (8, BLOCK))
            grad_queries, grad_keys, grad_values = attend_back(
                query_ref[here, lanes], grad, keys, values, keys_across,
                lse_ref[head, 0:1, here], inner,
            )
            grad_query_ref[lanes, here] = grad_queries.astype(BF16)
            total_keys = grad_keys if total_keys is None else total_keys + grad_keys
            total_values = grad_values if total_values is None else total_values + grad_values
        total_keys = (total_keys * SCALE).astype(BF16)
        total_values = total_values.astype(BF16)
        start = 0
        for ref in grad_far:
            count = ref.shape[1]
            ref[0, :, lanes] = total_keys[start : start + count]
            ref[1, :, lanes] = total_values[start : start + count]
            start += count


def far_backward(queries, far, mixed, grad_mixed, lse):
    rows, features = queries.shape
    heads = step_heads(features)
    width = heads * HEAD_DIM
    far_specs = [pair(part.shape[1], width) for part in far]
    return pl.pallas_call(
        functools.partial(far_back_kernel, len(far)),
        grid=(features // width,),
        in_specs=[column(rows, width)] * 3 + [stat(rows, heads)] + far_specs,
        out_specs=far_specs + [row(rows, width), stat(rows, heads)],
        out_shape=[jax.ShapeDtypeStruct(part.shape, BF16) for part in far]
        + [
            jax.ShapeDtypeStruct((features, rows), BF16),
            jax.ShapeDtypeStruct((features // HEAD_DIM, 8, rows), F32),
        ],
        compiler_params=params(WIDE_VMEM),
        cost_estimate=cost(14, queries),
        name="far_backward",
    )(queries, mixed, grad_mixed, lse, *far)


def near_back_kernel(
    local, parts, query_ref, key_ref, value_ref, coarse_ref, grad_ref, lse_ref, inner_ref,
    far_query_ref, *refs,
):
    far, (grad_query_ref, grad_key_ref, grad_value_ref) = refs[:parts], refs[-3:]
    rows = query_ref.shape[0]
    blocks = rows // BLOCK
    matrix = widen_matrix(BLOCK, POOLED, 1)
    for head, lanes in enumerate(lanes_of(query_ref)):
        keys, values = key_ref[:, lanes], value_ref[:, lanes]
        coarse_keys, coarse_values = coarse_ref[0, :, lanes], coarse_ref[1, :, lanes]
        keys_across, coarse_across = keys.T, coarse_keys.T
        own = [[None] * blocks, [None] * blocks]
        pooled = [[[None] * (blocks >> (level - 1)) for level in range(1, local)] for _ in range(2)]
        for index in range(2):
            held = None
            for part in far[::-1]:
                value = part[index, :, lanes].astype(F32)
                if held is not None:
                    wider = widen_matrix(value.shape[0], held.shape[0], 1)
                    value = value + nn(wider, held.astype(BF16))
                held = value
            pooled[index].append([held])
        for block, here in enumerate(blocks_of(query_ref)):
            starts = local_starts(block, local, rows)
            across = [keys_across[:, here]] + [coarse_across[:, at : at + POOLED] for at in starts]
            grad_queries, grad_keys, grad_values = attend_back(
                query_ref[here, lanes], grad_ref[here, lanes],
                local_list(keys, coarse_keys, block, local),
                local_list(values, coarse_values, block, local),
                jnp.concatenate(across, axis=1),
                lse_ref[head, 0:1, here], inner_ref[head, 0:1, here],
            )
            grad_queries = (grad_queries + far_query_ref[lanes, here].astype(F32)) * SCALE
            grad_query_ref[here, lanes] = grad_queries.T.astype(BF16)
            for index, value in enumerate((grad_keys * SCALE, grad_values)):
                own[index][block] = value[:BLOCK]
                for level in range(1, local):
                    sibling = block >> (level - 1) ^ 1
                    start = BLOCK + (level - 1) * POOLED
                    piece = value[start : start + POOLED]
                    held = pooled[index][level - 1]
                    held[sibling] = piece if held[sibling] is None else held[sibling] + piece
        for index, ref in enumerate((grad_key_ref, grad_value_ref)):
            for level in range(local, 0, -1):
                for half in range(len(pooled[index][level - 1])):
                    wide = nn(matrix, pooled[index][level - 1][half].astype(BF16))
                    if level == 1:
                        own[index][half] = own[index][half] + wide
                    else:
                        below = pooled[index][level - 2]
                        below[2 * half] = below[2 * half] + wide[:POOLED]
                        below[2 * half + 1] = below[2 * half + 1] + wide[POOLED:]
            for block, here in enumerate(blocks_of(query_ref)):
                ref[here, lanes] = own[index][block].astype(BF16)


def near_backward(operands, grads, local, part, parts):
    queries, coarse, pooled = operands[0], operands[3], operands[8:]
    rows, features = queries.shape
    heads = step_heads(features)
    width = heads * HEAD_DIM
    steps = features // width // parts
    first = part * steps

    def wide(count):
        return pl.BlockSpec((count, width), lambda h: (0, first + h))

    def pair_at(count):
        return pl.BlockSpec((2, count, width), lambda h: (0, 0, first + h))

    stats = pl.BlockSpec((heads, 8, rows), lambda h: (first + h, 0, 0))
    across = pl.BlockSpec((width, rows), lambda h: (first + h, 0))
    count = len(operands)
    return pl.pallas_call(
        functools.partial(near_back_kernel, local, len(pooled)),
        grid=(steps,),
        in_specs=[wide(rows)] * 3
        + [pair_at(coarse.shape[1]), wide(rows), stats, stats, across]
        + [pair_at(rows_of.shape[1]) for rows_of in pooled]
        + [pl.BlockSpec(memory_space=pl.ANY)] * len(grads),
        out_specs=[wide(rows)] * 3,
        out_shape=[jax.ShapeDtypeStruct((rows, features), BF16)] * 3,
        input_output_aliases={count + index: index for index in range(len(grads))},
        compiler_params=params(),
        cost_estimate=cost(18 / parts, queries),
        name="near_backward",
    )(*operands, *grads)


def index_call(
    kernel, name, micros, scalars, grid, in_specs, out_spec, out_shape, args, limit=VMEM, aliases={}
):
    return pl.pallas_call(
        kernel,
        grid_spec=pltpu.PrefetchScalarGridSpec(
            num_scalar_prefetch=1, grid=grid, in_specs=in_specs, out_specs=out_spec
        ),
        out_shape=out_shape,
        compiler_params=params(limit),
        input_output_aliases=aliases,
        cost_estimate=cost(micros, args[0]),
        name=name,
    )(scalars, *args)


def project_kernel(which_ref, mixed_ref, weight_ref, *refs):
    share = nn(mixed_ref[...], weight_ref[...]).astype(BF16)
    if len(refs) == 2:
        share = (share.astype(F32) + refs[0][...].astype(F32)).astype(BF16)
    refs[-1][...] = share


def project(mixed, out_weight, which, arrived=None):
    rows, features = mixed.shape
    width = min(512, features)
    steps = features // width
    out = pl.BlockSpec((rows, width), lambda j, which: (0, j))
    return index_call(
        project_kernel, "project", 5, which, (steps,),
        [
            pl.BlockSpec((rows, features), lambda j, which: (0, 0)),
            pl.BlockSpec((features, width), lambda j, which: (0, which[0] * steps + j)),
        ]
        + ([] if arrived is None else [out]),
        out, jax.ShapeDtypeStruct((rows, features), BF16),
        (mixed, out_weight) if arrived is None else (mixed, out_weight, arrived),
        limit=WIDE_VMEM,
    )


def mix_back_kernel(which_ref, own_ref, other_ref, own_weight_ref, other_weight_ref, out_ref):
    total = nt(own_ref[...], own_weight_ref[...]) + nt(other_ref[...], other_weight_ref[...])
    out_ref[...] = total.astype(BF16)


def mix_back(own, other, out_weight, which):
    rows, features = own.shape
    width = min(512, features)
    whole = pl.BlockSpec((rows, features), lambda j, which: (0, 0))
    return index_call(
        mix_back_kernel, "mix_back", 8, which, (features // width,),
        [
            whole,
            whole,
            pl.BlockSpec((width, features), lambda j, which: (j, which[0])),
            pl.BlockSpec((width, features), lambda j, which: (j, 1 - which[0])),
        ],
        pl.BlockSpec((rows, width), lambda j, which: (0, j)),
        jax.ShapeDtypeStruct((rows, features), BF16),
        (own, other, out_weight, out_weight),
    )


def weight_kernel(which_ref, mixed_ref, grad_ref, mine_ref, sent_ref):
    share = tn(mixed_ref[...], grad_ref[...]).astype(BF16)

    @pl.when(pl.program_id(0) == 0)
    def first():
        sent_ref[...] = share

    @pl.when(pl.program_id(0) == 1)
    def second():
        mine_ref[...] = share


def weight_halves(mixed, grad, which):
    rows, features = mixed.shape
    half = features // 2
    columns = grad.shape[1]
    steps = max(columns // 512, 1)
    width = columns // steps

    def mine_index(i, j, which):
        return 0, jnp.where(i == 1, j, 0)

    def sent_index(i, j, which):
        return 0, jnp.where(i == 0, j, steps - 1)

    return index_call(
        weight_kernel, "weight_halves", 4, which[None], (2, steps),
        [
            pl.BlockSpec((rows, half), lambda i, j, which: (0, 1 - i ^ which[0])),
            pl.BlockSpec((rows, width), lambda i, j, which: (0, j)),
        ],
        [pl.BlockSpec((half, width), mine_index), pl.BlockSpec((half, width), sent_index)],
        [jax.ShapeDtypeStruct((half, columns), BF16)] * 2, (mixed, grad),
    )


def add_kernel(which_ref, first_ref, second_ref, mine_ref, sent_ref):
    total = added(first_ref[...], second_ref[...])

    @pl.when(pl.program_id(0) == 0)
    def first():
        sent_ref[...] = total

    @pl.when(pl.program_id(0) == 1)
    def second():
        mine_ref[...] = total


def add_halves(first, second, which, micros):
    rows, columns = first.shape
    half = rows // 2
    spec = pl.BlockSpec((half, columns), lambda j, which: (1 - j ^ which[0], 0))
    out = pl.BlockSpec((half, columns), lambda j, which: (0, 0))
    return index_call(
        add_kernel, "add_halves", micros, which[None], (2,), [spec, spec], [out, out],
        [jax.ShapeDtypeStruct((half, columns), BF16)] * 2, (first, second), limit=WIDE_VMEM,
    )


def place_kernel(chunks, where_ref, first_ref, second_ref, *refs):
    out_ref = refs[-1]
    for index, ref in enumerate((first_ref, second_ref)):

        @pl.when(pl.program_id(0) == index)
        def copy(index=index, ref=ref):
            size = ref.shape[0] // chunks
            for chunk in range(chunks):
                start = pl.multiple_of((chunk ^ where_ref[0]) * size, size)
                out_ref[pl.ds(start, size), :] = ref[chunk * size : (chunk + 1) * size, :]


def place(first, second, chunks, where, held=None):
    half, columns = first.shape
    spec = pl.BlockSpec((half, columns), lambda step, where: (0, 0))
    return index_call(
        functools.partial(place_kernel, chunks), "place", 2, where, (2,),
        [spec, spec] + ([] if held is None else [pl.BlockSpec(memory_space=pl.ANY)]),
        pl.BlockSpec((half, columns), lambda step, where: (step ^ where[1], where[2])),
        jax.ShapeDtypeStruct((2 * half, 2 * columns), BF16),
        (first, second) if held is None else (first, second, held),
        aliases={} if held is None else {3: 0},
    )


def gather_far(pooled, meanwhile):
    cross = len(pooled)
    first, *chunks = [from_partner(rows, bit) for bit, rows in enumerate(pooled)]
    for bit in range(1, cross - 1):
        sizes = [chunk.shape[1] for chunk in chunks[bit:]]
        sent = jnp.concatenate(chunks[bit:], axis=1)
        if bit == 1:
            sent = tie(sent, meanwhile)
        arrived = from_partner(sent, bit)
        start = 0
        for index, size in enumerate(sizes):
            chunks[bit + index] = jnp.concatenate(
                [chunks[bit + index], arrived[:, start : start + size]], axis=1
            )
            start += size
    kept = jnp.concatenate(chunks, axis=1)
    return first, kept, from_partner(kept, 0)


def scatter_far(grad_first, grad_kept, grad_swapped, cross):
    parts = [from_partner(grad_first, 0)]
    arrived, after = yield move(grad_swapped, 0)
    kept = added(tie(grad_kept, *after), arrived)
    half = POOLED // 2
    chunks = [kept[:, index * half : (index + 1) * half] for index in range(cross - 1)]
    for bit in range(cross - 2, 0, -1):
        sizes = [chunk.shape[1] // 2 for chunk in chunks[bit:]]
        sent = jnp.concatenate([chunk[:, chunk.shape[1] // 2 :] for chunk in chunks[bit:]], axis=1)
        arrived, after = yield move(sent, bit, chunks[-1])
        chunks = list(tie(tuple(chunks), *after))
        start = 0
        for index, size in enumerate(sizes):
            chunks[bit + index] = added(
                chunks[bit + index][:, :size], arrived[:, start : start + size]
            )
            start += size
    parts += [from_partner(chunk, bit + 1) for bit, chunk in enumerate(chunks)]
    yield chunks[-1], tuple(parts)


def move(rows, bit, kept=None):
    return rows if kept is None else kept, from_partner(rows, bit)


def seq_bit(bit):
    return lax.axis_index("seq") >> bit & 1


def sum_rows(mine, sent, bits, micros):
    arrived, after = yield move(sent, 0, mine)
    for bit in bits[:-1]:
        mine, sent = add_halves(tie(mine, *after), arrived, seq_bit(bit), micros if after else 1)
        arrived, after = yield move(sent, bit, mine)
    rows = added(tie(mine, *after), arrived)
    arrived, after = yield move(rows, bits[-1])
    rows = added(tie(rows, *after), arrived)
    for bit in bits[-2::-1]:
        arrived, after = yield move(rows, bit)
        rows = jnp.concatenate([tie(rows, *after), arrived], axis=0)
    yield rows, move(rows, 0)


class Chain:
    def __init__(self, steps, count):
        self.steps, self.left = steps, count
        self.kept, self.moving = next(steps)

    def advance(self, *after):
        self.left -= 1
        self.kept, self.moving = self.steps.send((self.moving, after))


def chunk_index(bits):
    index = 0
    for bit in bits[:-1]:
        index = index * 2 + seq_bit(bit)
    return index


def solution_body(queries, key_states, value_states, out_weight, cotangent):
    rows, features = queries.shape
    cross = lax.axis_size("seq").bit_length() - 1
    local = (rows // POOLED).bit_length() - 1
    groups = lax.axis_size("head")
    group = lax.axis_index("head")
    swap = [(0, 1), (1, 0)]
    if groups == 2:
        other = lax.ppermute(cotangent, "head", swap)
    else:
        piece = lax.all_gather(cotangent, "head", axis=1, tiled=True)
    coarse, *pooled = pool(key_states, value_states, local, cross)
    near, near_lse = near_forward(queries, key_states, value_states, coarse, local)
    far = gather_far(pooled, near)
    mixed, lse = far_forward(queries, far, near, near_lse)
    if groups == 2:
        share = project(mixed, out_weight, (1 - group)[None])
        shared = lax.ppermute(share, "head", swap)
        first, second, flip = tie(cotangent, share), other, group
    else:
        partial_out = jnp.dot(mixed, out_weight, preferred_element_type=F32).astype(BF16)
        attended = lax.psum_scatter(partial_out, "head", scatter_dimension=1, tiled=True)
        grad_mixed = nt(piece, out_weight).astype(BF16)
        middle = piece.shape[1] // 2
        first, second, flip = piece[:, :middle], piece[:, middle:], 0
    first_bits = list(range(1, cross))
    second_bits = first_bits[1:] + first_bits[:1]
    first_halves = weight_halves(mixed, first, seq_bit(0))
    first_sum = Chain(sum_rows(*first_halves, first_bits, 1), 2 * cross - 2)
    second_halves = weight_halves(mixed, tie(second, *first_halves), seq_bit(0))
    second_sum = Chain(sum_rows(*second_halves, second_bits, 200), 2 * cross - 2)
    first_sum.advance()
    second_sum.advance()
    if groups == 2:
        ready = tie(cotangent, first_sum.kept, second_sum.kept)
        grad_mixed = mix_back(ready, other, out_weight, group[None])
    *grad_far, far_query, inner = far_backward(queries, far, mixed, grad_mixed, lse)
    far_sum = Chain(scatter_far(*grad_far, cross), cross - 1)
    first_sum.advance(inner)
    second_sum.advance(inner)
    arrivals = (shared,) if groups == 2 else ()
    far_sum.advance(first_sum.kept, second_sum.kept, *arrivals)
    if groups == 2:
        attended = project(tie(mixed, far_sum.kept), out_weight, group[None], shared)
    far_sum.advance(*([attended] if groups == 2 else []))
    first_sum.advance(far_sum.kept)
    while far_sum.left:
        far_sum.advance(first_sum.kept)
    second_sum.advance(far_sum.kept)
    first_sum.advance(second_sum.kept, *far_sum.moving)
    second_sum.advance(*far_sum.moving)
    inner = tie(inner, first_sum.kept, second_sum.kept)
    operands = (
        queries, key_states, value_states, coarse, grad_mixed, lse, inner, far_query,
        *far_sum.moving,
    )
    parts = 2 if features % (4 * HEAD_DIM) == 0 else 1
    grads = ()
    for part in range(parts):
        grads = near_backward(operands, grads, local, part, parts)
        if first_sum.left:
            first_sum.advance(grads[0])
            second_sum.advance(grads[0])
    grad_queries, grad_keys, grad_values = grads
    for chain in (first_sum, second_sum):
        while chain.left:
            chain.advance()
    core = seq_bit(0)
    flip = jnp.asarray(flip, jnp.int32)
    chunks = 1 << (cross - 2)
    grad_weight = place(
        *first_sum.moving, chunks, jnp.stack([chunk_index(first_bits), core, flip])
    )
    grad_weight = place(
        *second_sum.moving, chunks, jnp.stack([chunk_index(second_bits), core, 1 - flip]),
        grad_weight,
    )
    return attended, grad_queries, grad_keys, grad_values, grad_weight


def solution(mesh):
    split = P("seq", "head")
    return jax.shard_map(
        solution_body,
        mesh=mesh,
        in_specs=(split, split, split, P("head", None), split),
        out_specs=(split, split, split, split, P("head", None)),
        check_vma=False,
    )
```

```python
import functools

import jax
import jax.numpy as jnp
from jax import lax
from jax.experimental import pallas as pl
from jax.experimental.pallas import tpu as pltpu
from jax.sharding import PartitionSpec as P

HEAD_DIM = 128
BLOCK = 256
POOLED = 128
SCALE = HEAD_DIM ** -0.5
SCALE2 = SCALE * 1.4426950408889634
VMEM = 48 * 1024 * 1024
WIDE_VMEM = 60 * 1024 * 1024
F32 = jnp.float32
BF16 = jnp.bfloat16


def params(limit=VMEM):
    return pltpu.CompilerParams(vmem_limit_bytes=limit)


def cost(micros, like):
    scale = 0.05 * micros * like.shape[0] * like.shape[1] / (1 << 20)
    return pl.CostEstimate(
        flops=int(scale * 1.15e9), bytes_accessed=int(scale * 3.6e6), transcendentals=0
    )


def nn(a, b):
    return lax.dot_general(a, b, (((1,), (0,)), ((), ())), preferred_element_type=F32)


def nt(a, b):
    return lax.dot_general(a, b, (((1,), (1,)), ((), ())), preferred_element_type=F32)


def tn(a, b):
    return lax.dot_general(a, b, (((0,), (0,)), ((), ())), preferred_element_type=F32)


def widen_matrix(rows, columns, shift):
    row = lax.broadcasted_iota(jnp.int32, (rows, columns), 0)
    column = lax.broadcasted_iota(jnp.int32, (rows, columns), 1)
    return jnp.where((row >> shift) == column, 0.5 ** shift, 0.0).astype(BF16)


def added(first, second):
    return (first.astype(F32) + second.astype(F32)).astype(BF16)


def tie(value, *others):
    return lax.optimization_barrier((value, *others))[0] if others else value


def from_partner(block, bit):
    count = lax.axis_size("seq")
    return lax.ppermute(block, "seq", [(low, low ^ 1 << bit) for low in range(count)])


def column(rows, width):
    return pl.BlockSpec((rows, width), lambda h: (0, h))


def row(rows, width):
    return pl.BlockSpec((width, rows), lambda h: (h, 0))


def pair(rows, width):
    return pl.BlockSpec((2, rows, width), lambda h: (0, 0, h))


def stat(rows, heads):
    return pl.BlockSpec((heads, 8, rows), lambda h: (h, 0, 0))


def lanes_of(ref):
    return [slice(start, start + HEAD_DIM) for start in range(0, ref.shape[-1], HEAD_DIM)]


def blocks_of(ref):
    return [slice(start, start + BLOCK) for start in range(0, ref.shape[0], BLOCK)]


def step_heads(features, most=2):
    return min(features // HEAD_DIM, most)


def pool_kernel(local, cross, key_ref, value_ref, coarse_ref, *refs):
    pooled, held_ref = refs[:-1], refs[-1]
    for index, ref in enumerate((key_ref, value_ref)):
        for head, lanes in enumerate(lanes_of(ref)):
            held = held_ref.at[index, head]
            count = ref.shape[0]
            coarse_start = 0
            held[...] = ref[:, lanes].astype(F32)
            for level in range(1, local + cross):
                count //= 2
                even = held[pl.ds(0, count, stride=2), :]
                odd = held[pl.ds(1, count, stride=2), :]
                rows = (0.5 * (even + odd)).astype(BF16)
                if level < local:
                    coarse_ref[index, coarse_start : coarse_start + count, lanes] = rows
                    coarse_start += count
                else:
                    pooled[level - local][index, :, lanes] = rows
                held[0:count, :] = rows.astype(F32)


def pool(key_states, value_states, local, cross):
    rows, features = key_states.shape
    heads = step_heads(features)
    width = heads * HEAD_DIM
    counts = [sum(rows >> level for level in range(1, local))]
    counts += [POOLED >> bit for bit in range(cross)]
    return pl.pallas_call(
        functools.partial(pool_kernel, local, cross),
        grid=(features // width,),
        in_specs=[column(rows, width)] * 2,
        out_specs=[pair(count, width) for count in counts],
        out_shape=[jax.ShapeDtypeStruct((2, count, features), BF16) for count in counts],
        scratch_shapes=[pltpu.VMEM((2, heads, rows, HEAD_DIM), F32)],
        compiler_params=params(WIDE_VMEM),
        cost_estimate=cost(5, key_states),
        name="pool",
    )(key_states, value_states)


def local_starts(block, local, rows):
    starts = []
    offset = 0
    for level in range(1, local):
        starts.append(offset + (block >> (level - 1) ^ 1) * POOLED)
        offset += rows >> level
    return starts


def local_list(own, coarse, block, local):
    parts = [own[block * BLOCK : (block + 1) * BLOCK]]
    parts += [coarse[at : at + POOLED] for at in local_starts(block, local, own.shape[0])]
    return jnp.concatenate(parts, axis=0)


def lane_max(scores):
    count = scores.shape[1]
    while count > HEAD_DIM:
        half = (count // HEAD_DIM + 1) // 2 * HEAD_DIM
        top = jnp.maximum(scores[:, : count - half], scores[:, half:])
        if 2 * half > count:
            top = jnp.concatenate([top, scores[:, count - half : half]], axis=1)
        scores, count = top, half
    return jnp.max(scores, axis=1, keepdims=True)


def attend(queries, keys, values):
    scores = nt(queries, keys)
    top = lane_max(scores)
    weights = jnp.exp2((scores - top) * SCALE2).astype(BF16)
    ones = jnp.ones((values.shape[0], HEAD_DIM), BF16)
    mixed = nn(weights, jnp.concatenate([values, ones], axis=1))
    total = mixed[:, HEAD_DIM:]
    return mixed[:, :HEAD_DIM] / total, top * SCALE2 + jnp.log2(total)


def near_kernel(local, query_ref, key_ref, value_ref, coarse_ref, out_ref, lse_ref):
    for head, lanes in enumerate(lanes_of(query_ref)):
        keys, values = key_ref[:, lanes], value_ref[:, lanes]
        coarse_keys, coarse_values = coarse_ref[0, :, lanes], coarse_ref[1, :, lanes]
        for block, here in enumerate(blocks_of(query_ref)):
            mixed, lse = attend(
                query_ref[here, lanes],
                local_list(keys, coarse_keys, block, local),
                local_list(values, coarse_values, block, local),
            )
            out_ref[here, lanes] = mixed.astype(BF16)
            lse_ref[head, :, here] = lse.T[:8]


def far_kernel(parts, query_ref, *refs):
    far, (near_ref, near_lse_ref, mixed_ref, lse_ref) = refs[:parts], refs[parts:]
    for head, lanes in enumerate(lanes_of(query_ref)):
        keys = jnp.concatenate([part[0, :, lanes] for part in far], axis=0)
        values = jnp.concatenate([part[1, :, lanes] for part in far], axis=0)
        for here in blocks_of(query_ref):
            mixed, lse = attend(query_ref[here, lanes], keys, values)
            near_lse = jnp.broadcast_to(near_lse_ref[head, 0:1, here], (HEAD_DIM, BLOCK)).T
            top = jnp.maximum(near_lse, lse)
            near_share = jnp.exp2(near_lse - top)
            far_share = jnp.exp2(lse - top)
            total = near_share + far_share
            both = near_ref[here, lanes].astype(F32) * near_share + mixed * far_share
            mixed_ref[here, lanes] = (both / total).astype(BF16)
            lse_ref[head, :, here] = (top + jnp.log2(total)).T[:8]


def near_forward(queries, key_states, value_states, coarse, local):
    rows, features = queries.shape
    heads = step_heads(features, 4)
    width = heads * HEAD_DIM
    return pl.pallas_call(
        functools.partial(near_kernel, local),
        grid=(features // width,),
        in_specs=[column(rows, width)] * 3 + [pair(coarse.shape[1], width)],
        out_specs=[column(rows, width), stat(rows, heads)],
        out_shape=[
            jax.ShapeDtypeStruct((rows, features), BF16),
            jax.ShapeDtypeStruct((features // HEAD_DIM, 8, rows), F32),
        ],
        compiler_params=params(),
        cost_estimate=cost(9, queries),
        name="near_forward",
    )(queries, key_states, value_states, coarse)


def far_forward(queries, far, near, near_lse):
    rows, features = queries.shape
    heads = step_heads(features)
    width = heads * HEAD_DIM
    return pl.pallas_call(
        functools.partial(far_kernel, len(far)),
        grid=(features // width,),
        in_specs=[column(rows, width)]
        + [pair(part.shape[1], width) for part in far]
        + [column(rows, width), stat(rows, heads)],
        out_specs=[column(rows, width), stat(rows, heads)],
        out_shape=[
            jax.ShapeDtypeStruct((rows, features), BF16),
            jax.ShapeDtypeStruct((features // HEAD_DIM, 8, rows), F32),
        ],
        compiler_params=params(WIDE_VMEM),
        cost_estimate=cost(10, queries),
        name="far_forward",
    )(queries, *far, near, near_lse)


def attend_back(queries, grad_mixed, keys, values, keys_across, lse, inner):
    weights = jnp.exp2(nt(keys, queries) * SCALE2 - lse)
    grad_probs = nt(values, grad_mixed)
    grad_scores = (weights * (grad_probs - inner)).astype(BF16)
    both = jnp.concatenate([grad_mixed, queries], axis=1)
    grad_values = nn(weights.astype(BF16), both)[:, :HEAD_DIM]
    grad_keys = nn(grad_scores, both)[:, HEAD_DIM:]
    return nn(keys_across, grad_scores), grad_keys, grad_values


def far_back_kernel(parts, query_ref, mixed_ref, grad_ref, lse_ref, *refs):
    far, grad_far = refs[:parts], refs[parts : 2 * parts]
    grad_query_ref, inner_ref = refs[2 * parts :]
    for head, lanes in enumerate(lanes_of(query_ref)):
        keys = jnp.concatenate([part[0, :, lanes] for part in far], axis=0)
        values = jnp.concatenate([part[1, :, lanes] for part in far], axis=0)
        keys_across = keys.T
        total_keys = total_values = None
        for here in blocks_of(query_ref):
            grad = grad_ref[here, lanes]
            product = (grad.astype(F32) * mixed_ref[here, lanes].astype(F32)).T
            inner = jnp.sum(product, axis=0, keepdims=True)
            inner_ref[head, :, here] = jnp.broadcast_to(inner, (8, BLOCK))
            grad_queries, grad_keys, grad_values = attend_back(
                query_ref[here, lanes], grad, keys, values, keys_across,
                lse_ref[head, 0:1, here], inner,
            )
            grad_query_ref[lanes, here] = grad_queries.astype(BF16)
            total_keys = grad_keys if total_keys is None else total_keys + grad_keys
            total_values = grad_values if total_values is None else total_values + grad_values
        total_keys = (total_keys * SCALE).astype(BF16)
        total_values = total_values.astype(BF16)
        start = 0
        for ref in grad_far:
            count = ref.shape[1]
            ref[0, :, lanes] = total_keys[start : start + count]
            ref[1, :, lanes] = total_values[start : start + count]
            start += count


def far_backward(queries, far, mixed, grad_mixed, lse):
    rows, features = queries.shape
    heads = step_heads(features)
    width = heads * HEAD_DIM
    far_specs = [pair(part.shape[1], width) for part in far]
    return pl.pallas_call(
        functools.partial(far_back_kernel, len(far)),
        grid=(features // width,),
        in_specs=[column(rows, width)] * 3 + [stat(rows, heads)] + far_specs,
        out_specs=far_specs + [row(rows, width), stat(rows, heads)],
        out_shape=[jax.ShapeDtypeStruct(part.shape, BF16) for part in far]
        + [
            jax.ShapeDtypeStruct((features, rows), BF16),
            jax.ShapeDtypeStruct((features // HEAD_DIM, 8, rows), F32),
        ],
        compiler_params=params(WIDE_VMEM),
        cost_estimate=cost(14, queries),
        name="far_backward",
    )(queries, mixed, grad_mixed, lse, *far)


def near_back_kernel(
    local, parts, query_ref, key_ref, value_ref, coarse_ref, grad_ref, lse_ref, inner_ref,
    far_query_ref, *refs,
):
    far, (grad_query_ref, grad_key_ref, grad_value_ref) = refs[:parts], refs[-3:]
    rows = query_ref.shape[0]
    blocks = rows // BLOCK
    matrix = widen_matrix(BLOCK, POOLED, 1)
    for head, lanes in enumerate(lanes_of(query_ref)):
        keys, values = key_ref[:, lanes], value_ref[:, lanes]
        coarse_keys, coarse_values = coarse_ref[0, :, lanes], coarse_ref[1, :, lanes]
        keys_across, coarse_across = keys.T, coarse_keys.T
        own = [[None] * blocks, [None] * blocks]
        pooled = [[[None] * (blocks >> (level - 1)) for level in range(1, local)] for _ in range(2)]
        for index in range(2):
            held = None
            for part in far[::-1]:
                value = part[index, :, lanes].astype(F32)
                if held is not None:
                    wider = widen_matrix(value.shape[0], held.shape[0], 1)
                    value = value + nn(wider, held.astype(BF16))
                held = value
            pooled[index].append([held])
        for block, here in enumerate(blocks_of(query_ref)):
            starts = local_starts(block, local, rows)
            across = [keys_across[:, here]] + [coarse_across[:, at : at + POOLED] for at in starts]
            grad_queries, grad_keys, grad_values = attend_back(
                query_ref[here, lanes], grad_ref[here, lanes],
                local_list(keys, coarse_keys, block, local),
                local_list(values, coarse_values, block, local),
                jnp.concatenate(across, axis=1),
                lse_ref[head, 0:1, here], inner_ref[head, 0:1, here],
            )
            grad_queries = (grad_queries + far_query_ref[lanes, here].astype(F32)) * SCALE
            grad_query_ref[here, lanes] = grad_queries.T.astype(BF16)
            for index, value in enumerate((grad_keys * SCALE, grad_values)):
                own[index][block] = value[:BLOCK]
                for level in range(1, local):
                    sibling = block >> (level - 1) ^ 1
                    start = BLOCK + (level - 1) * POOLED
                    piece = value[start : start + POOLED]
                    held = pooled[index][level - 1]
                    held[sibling] = piece if held[sibling] is None else held[sibling] + piece
        for index, ref in enumerate((grad_key_ref, grad_value_ref)):
            for level in range(local, 0, -1):
                for half in range(len(pooled[index][level - 1])):
                    wide = nn(matrix, pooled[index][level - 1][half].astype(BF16))
                    if level == 1:
                        own[index][half] = own[index][half] + wide
                    else:
                        below = pooled[index][level - 2]
                        below[2 * half] = below[2 * half] + wide[:POOLED]
                        below[2 * half + 1] = below[2 * half + 1] + wide[POOLED:]
            for block, here in enumerate(blocks_of(query_ref)):
                ref[here, lanes] = own[index][block].astype(BF16)


def near_backward(operands, grads, local, part, parts):
    queries, coarse, pooled = operands[0], operands[3], operands[8:]
    rows, features = queries.shape
    heads = step_heads(features)
    width = heads * HEAD_DIM
    steps = features // width // parts
    first = part * steps

    def wide(count):
        return pl.BlockSpec((count, width), lambda h: (0, first + h))

    def pair_at(count):
        return pl.BlockSpec((2, count, width), lambda h: (0, 0, first + h))

    stats = pl.BlockSpec((heads, 8, rows), lambda h: (first + h, 0, 0))
    across = pl.BlockSpec((width, rows), lambda h: (first + h, 0))
    count = len(operands)
    return pl.pallas_call(
        functools.partial(near_back_kernel, local, len(pooled)),
        grid=(steps,),
        in_specs=[wide(rows)] * 3
        + [pair_at(coarse.shape[1]), wide(rows), stats, stats, across]
        + [pair_at(rows_of.shape[1]) for rows_of in pooled]
        + [pl.BlockSpec(memory_space=pl.ANY)] * len(grads),
        out_specs=[wide(rows)] * 3,
        out_shape=[jax.ShapeDtypeStruct((rows, features), BF16)] * 3,
        input_output_aliases={count + index: index for index in range(len(grads))},
        compiler_params=params(),
        cost_estimate=cost(18 / parts, queries),
        name="near_backward",
    )(*operands, *grads)


def index_call(
    kernel, name, micros, scalars, grid, in_specs, out_spec, out_shape, args, limit=VMEM, aliases={}
):
    return pl.pallas_call(
        kernel,
        grid_spec=pltpu.PrefetchScalarGridSpec(
            num_scalar_prefetch=1, grid=grid, in_specs=in_specs, out_specs=out_spec
        ),
        out_shape=out_shape,
        compiler_params=params(limit),
        input_output_aliases=aliases,
        cost_estimate=cost(micros, args[0]),
        name=name,
    )(scalars, *args)


def project_kernel(which_ref, mixed_ref, weight_ref, *refs):
    share = nn(mixed_ref[...], weight_ref[...]).astype(BF16)
    if len(refs) == 2:
        share = (share.astype(F32) + refs[0][...].astype(F32)).astype(BF16)
    refs[-1][...] = share


def project(mixed, out_weight, which, arrived=None):
    rows, features = mixed.shape
    width = min(512, features)
    steps = features // width
    out = pl.BlockSpec((rows, width), lambda j, which: (0, j))
    return index_call(
        project_kernel, "project", 5, which, (steps,),
        [
            pl.BlockSpec((rows, features), lambda j, which: (0, 0)),
            pl.BlockSpec((features, width), lambda j, which: (0, which[0] * steps + j)),
        ]
        + ([] if arrived is None else [out]),
        out, jax.ShapeDtypeStruct((rows, features), BF16),
        (mixed, out_weight) if arrived is None else (mixed, out_weight, arrived),
        limit=WIDE_VMEM,
    )


def mix_back_kernel(which_ref, own_ref, other_ref, own_weight_ref, other_weight_ref, out_ref):
    total = nt(own_ref[...], own_weight_ref[...]) + nt(other_ref[...], other_weight_ref[...])
    out_ref[...] = total.astype(BF16)


def mix_back(own, other, out_weight, which):
    rows, features = own.shape
    width = min(512, features)
    whole = pl.BlockSpec((rows, features), lambda j, which: (0, 0))
    return index_call(
        mix_back_kernel, "mix_back", 8, which, (features // width,),
        [
            whole,
            whole,
            pl.BlockSpec((width, features), lambda j, which: (j, which[0])),
            pl.BlockSpec((width, features), lambda j, which: (j, 1 - which[0])),
        ],
        pl.BlockSpec((rows, width), lambda j, which: (0, j)),
        jax.ShapeDtypeStruct((rows, features), BF16),
        (own, other, out_weight, out_weight),
    )


def weight_kernel(which_ref, mixed_ref, grad_ref, mine_ref, sent_ref):
    share = tn(mixed_ref[...], grad_ref[...]).astype(BF16)

    @pl.when(pl.program_id(0) == 0)
    def first():
        sent_ref[...] = share

    @pl.when(pl.program_id(0) == 1)
    def second():
        mine_ref[...] = share


def weight_halves(mixed, grad, which):
    rows, features = mixed.shape
    half = features // 2
    columns = grad.shape[1]
    steps = max(columns // 512, 1)
    width = columns // steps

    def mine_index(i, j, which):
        return 0, jnp.where(i == 1, j, 0)

    def sent_index(i, j, which):
        return 0, jnp.where(i == 0, j, steps - 1)

    return index_call(
        weight_kernel, "weight_halves", 4, which[None], (2, steps),
        [
            pl.BlockSpec((rows, half), lambda i, j, which: (0, 1 - i ^ which[0])),
            pl.BlockSpec((rows, width), lambda i, j, which: (0, j)),
        ],
        [pl.BlockSpec((half, width), mine_index), pl.BlockSpec((half, width), sent_index)],
        [jax.ShapeDtypeStruct((half, columns), BF16)] * 2, (mixed, grad),
    )


def add_kernel(which_ref, first_ref, second_ref, mine_ref, sent_ref):
    total = added(first_ref[...], second_ref[...])

    @pl.when(pl.program_id(0) == 0)
    def first():
        sent_ref[...] = total

    @pl.when(pl.program_id(0) == 1)
    def second():
        mine_ref[...] = total


def add_halves(first, second, which, micros):
    rows, columns = first.shape
    half = rows // 2
    spec = pl.BlockSpec((half, columns), lambda j, which: (1 - j ^ which[0], 0))
    out = pl.BlockSpec((half, columns), lambda j, which: (0, 0))
    return index_call(
        add_kernel, "add_halves", micros, which[None], (2,), [spec, spec], [out, out],
        [jax.ShapeDtypeStruct((half, columns), BF16)] * 2, (first, second), limit=WIDE_VMEM,
    )


def place_kernel(chunks, where_ref, first_ref, second_ref, *refs):
    out_ref = refs[-1]
    for index, ref in enumerate((first_ref, second_ref)):

        @pl.when(pl.program_id(0) == index)
        def copy(index=index, ref=ref):
            size = ref.shape[0] // chunks
            for chunk in range(chunks):
                start = pl.multiple_of((chunk ^ where_ref[0]) * size, size)
                out_ref[pl.ds(start, size), :] = ref[chunk * size : (chunk + 1) * size, :]


def place(first, second, chunks, where, held=None):
    half, columns = first.shape
    spec = pl.BlockSpec((half, columns), lambda step, where: (0, 0))
    return index_call(
        functools.partial(place_kernel, chunks), "place", 2, where, (2,),
        [spec, spec] + ([] if held is None else [pl.BlockSpec(memory_space=pl.ANY)]),
        pl.BlockSpec((half, columns), lambda step, where: (step ^ where[1], where[2])),
        jax.ShapeDtypeStruct((2 * half, 2 * columns), BF16),
        (first, second) if held is None else (first, second, held),
        aliases={} if held is None else {3: 0},
    )


def gather_far(pooled, meanwhile):
    cross = len(pooled)
    first, *chunks = [from_partner(rows, bit) for bit, rows in enumerate(pooled)]
    for bit in range(1, cross - 1):
        sizes = [chunk.shape[1] for chunk in chunks[bit:]]
        sent = jnp.concatenate(chunks[bit:], axis=1)
        if bit == 1:
            sent = tie(sent, meanwhile)
        arrived = from_partner(sent, bit)
        start = 0
        for index, size in enumerate(sizes):
            chunks[bit + index] = jnp.concatenate(
                [chunks[bit + index], arrived[:, start : start + size]], axis=1
            )
            start += size
    kept = jnp.concatenate(chunks, axis=1)
    return first, kept, from_partner(kept, 0)


def scatter_far(grad_first, grad_kept, grad_swapped, cross):
    parts = [from_partner(grad_first, 0)]
    arrived, after = yield move(grad_swapped, 0)
    kept = added(tie(grad_kept, *after), arrived)
    half = POOLED // 2
    chunks = [kept[:, index * half : (index + 1) * half] for index in range(cross - 1)]
    for bit in range(cross - 2, 0, -1):
        sizes = [chunk.shape[1] // 2 for chunk in chunks[bit:]]
        sent = jnp.concatenate([chunk[:, chunk.shape[1] // 2 :] for chunk in chunks[bit:]], axis=1)
        arrived, after = yield move(sent, bit, chunks[-1])
        chunks = list(tie(tuple(chunks), *after))
        start = 0
        for index, size in enumerate(sizes):
            chunks[bit + index] = added(
                chunks[bit + index][:, :size], arrived[:, start : start + size]
            )
            start += size
    parts += [from_partner(chunk, bit + 1) for bit, chunk in enumerate(chunks)]
    yield chunks[-1], tuple(parts)


def move(rows, bit, kept=None):
    return rows if kept is None else kept, from_partner(rows, bit)


def seq_bit(bit):
    return lax.axis_index("seq") >> bit & 1


def sum_rows(mine, sent, bits, micros):
    arrived, after = yield move(sent, 0, mine)
    for bit in bits[:-1]:
        mine, sent = add_halves(tie(mine, *after), arrived, seq_bit(bit), micros if after else 1)
        arrived, after = yield move(sent, bit, mine)
    rows = added(tie(mine, *after), arrived)
    arrived, after = yield move(rows, bits[-1])
    rows = added(tie(rows, *after), arrived)
    for bit in bits[-2::-1]:
        arrived, after = yield move(rows, bit)
        rows = jnp.concatenate([tie(rows, *after), arrived], axis=0)
    yield rows, move(rows, 0)


class Chain:
    def __init__(self, steps, count):
        self.steps, self.left = steps, count
        self.kept, self.moving = next(steps)

    def advance(self, *after):
        self.left -= 1
        self.kept, self.moving = self.steps.send((self.moving, after))


def chunk_index(bits):
    index = 0
    for bit in bits[:-1]:
        index = index * 2 + seq_bit(bit)
    return index


def solution_body(queries, key_states, value_states, out_weight, cotangent):
    rows, features = queries.shape
    cross = lax.axis_size("seq").bit_length() - 1
    local = (rows // POOLED).bit_length() - 1
    groups = lax.axis_size("head")
    group = lax.axis_index("head")
    swap = [(0, 1), (1, 0)]
    if groups == 2:
        other = lax.ppermute(cotangent, "head", swap)
    else:
        piece = lax.all_gather(cotangent, "head", axis=1, tiled=True)
    coarse, *pooled = pool(key_states, value_states, local, cross)
    near, near_lse = near_forward(queries, key_states, value_states, coarse, local)
    far = gather_far(pooled, near)
    mixed, lse = far_forward(queries, far, near, near_lse)
    if groups == 2:
        share = project(mixed, out_weight, (1 - group)[None])
        shared = lax.ppermute(share, "head", swap)
        first, second, flip = tie(cotangent, share), other, group
    else:
        partial_out = jnp.dot(mixed, out_weight, preferred_element_type=F32).astype(BF16)
        attended = lax.psum_scatter(partial_out, "head", scatter_dimension=1, tiled=True)
        grad_mixed = nt(piece, out_weight).astype(BF16)
        middle = piece.shape[1] // 2
        first, second, flip = piece[:, :middle], piece[:, middle:], 0
    first_bits = list(range(1, cross))
    second_bits = first_bits[1:] + first_bits[:1]
    first_halves = weight_halves(mixed, first, seq_bit(0))
    first_sum = Chain(sum_rows(*first_halves, first_bits, 1), 2 * cross - 2)
    second_halves = weight_halves(mixed, tie(second, *first_halves), seq_bit(0))
    second_sum = Chain(sum_rows(*second_halves, second_bits, 200), 2 * cross - 2)
    first_sum.advance()
    second_sum.advance()
    if groups == 2:
        ready = tie(cotangent, first_sum.kept, second_sum.kept)
        grad_mixed = mix_back(ready, other, out_weight, group[None])
    *grad_far, far_query, inner = far_backward(queries, far, mixed, grad_mixed, lse)
    far_sum = Chain(scatter_far(*grad_far, cross), cross - 1)
    first_sum.advance(inner)
    second_sum.advance(inner)
    arrivals = (shared,) if groups == 2 else ()
    far_sum.advance(first_sum.kept, *arrivals)
    if groups == 2:
        attended = project(tie(mixed, far_sum.kept), out_weight, group[None], shared)
    far_sum.advance(*([attended] if groups == 2 else []))
    first_sum.advance(far_sum.kept)
    while far_sum.left:
        far_sum.advance(first_sum.kept)
    second_sum.advance(far_sum.kept)
    first_sum.advance(second_sum.kept, *far_sum.moving)
    second_sum.advance(*far_sum.moving)
    inner = tie(inner, first_sum.kept, second_sum.kept)
    operands = (
        queries, key_states, value_states, coarse, grad_mixed, lse, inner, far_query,
        *far_sum.moving,
    )
    parts = 2 if features % (4 * HEAD_DIM) == 0 else 1
    grads = ()
    for part in range(parts):
        grads = near_backward(operands, grads, local, part, parts)
        if first_sum.left:
            first_sum.advance(grads[0])
            second_sum.advance(grads[0])
    grad_queries, grad_keys, grad_values = grads
    for chain in (first_sum, second_sum):
        while chain.left:
            chain.advance()
    core = seq_bit(0)
    flip = jnp.asarray(flip, jnp.int32)
    chunks = 1 << (cross - 2)
    grad_weight = place(
        *first_sum.moving, chunks, jnp.stack([chunk_index(first_bits), core, flip])
    )
    grad_weight = place(
        *second_sum.moving, chunks, jnp.stack([chunk_index(second_bits), core, 1 - flip]),
        grad_weight,
    )
    return attended, grad_queries, grad_keys, grad_values, grad_weight


def solution(mesh):
    split = P("seq", "head")
    return jax.shard_map(
        solution_body,
        mesh=mesh,
        in_specs=(split, split, split, P("head", None), split),
        out_specs=(split, split, split, split, P("head", None)),
        check_vma=False,
    )
```
